512 devices in a mesh: row: 8 (over z_lo), col: 8 (over z_hi, y), depth: 8 (over x, core).
Axes of the slice: x: 4, y: 4, z: 16 (z_hi: 2, z_lo: 8; z = z_hi * 8 + z_lo), core: 2. Of those that a mesh axis runs over, the one named last changes fastest.
Arguments:
- tile_values: bfloat16 [8, 64, 64, 128, 128], P('row', ('col', 'depth')), may hold values from 0 to 0.019897461
- tile_rows: int32 [8, 64, 64], P('row', ('col', 'depth')), may hold values from 0 to 39, as said below
- tile_cols: int32 [8, 64, 64], P('row', ('col', 'depth')), may hold values from 0 to 4
- tile_count: int32 [8, 64], P('row', ('col', 'depth')), may hold values from 1 to 64, as said below
- features: bfloat16 [40960, 128], P(('col', 'depth')), may hold values from -6 to 6
- weight: bfloat16 [128, 256], replicated, may hold values from -0.5 to 0.5
- cotangent: bfloat16 [40960, 256], P(('row', 'col', 'depth')), may hold values from -6 to 6
Outputs:
- activations: bfloat16 [40960, 256], P(('row', 'col', 'depth'))
- input_grad: bfloat16 [64, 640, 128], P(('col', 'depth'), 'row')
- weight_grad: float32 [128, 256], replicated
The draws below stay inside these ranges and needn't reach their ends.
Inputs may be any that keep to these rules, and one draw needn't show every extreme that they name: Within one device the pairs (tile_rows, tile_cols) of all 64 slots are distinct. `tile_count`: some device holds 64 tiles in every draw.
All inputs are finite; a program needn't handle non-finite values.
Results may differ from the reference program's by a relative error of at most 0.019.
Values may be sent and summed in bfloat16 or wider, within the bound.
A program may use at most 64 MiB of HBM per device.

```python
import math
import jax
import jax.numpy as jnp
from jax import lax

TILE = 128
F = 128
HID = 256
RB = 40
TMAX = 64
CB = 5
NODES = 40960
N_ROW = 8
N_COL = 8
N_DEPTH = 8


def tile_positions(key):
    keys = jax.random.split(key, N_ROW * N_COL * N_DEPTH)
    orders = jax.vmap(lambda single: jax.random.permutation(single, RB * CB))(keys)
    return orders[:, :TMAX].reshape(N_ROW, N_COL * N_DEPTH, TMAX).astype(jnp.int32)


def draw_tile_rows(key, part):
    places = tile_positions(key)
    return (places // CB).astype(jnp.int32)


def draw_tile_cols(key, part):
    places = tile_positions(key)
    return (places % CB).astype(jnp.int32)


def draw_tile_count(key, part):
    key = jax.random.fold_in(key, 5)
    first, second, third = jax.random.split(key, 3)
    shape = (N_ROW, N_COL * N_DEPTH)
    base = jax.random.randint(first, shape, max(1, TMAX // 8), TMAX // 2 + 1)
    busy = jax.random.randint(second, shape, 0, 8) == 0
    chosen = jax.random.randint(third, (), 0, N_ROW * N_COL * N_DEPTH)
    flat_index = jnp.arange(N_ROW * N_COL * N_DEPTH, dtype=jnp.int32).reshape(shape)
    full = jnp.logical_or(busy, flat_index == chosen)
    return jnp.where(full, TMAX, base).astype(jnp.int32)


def levels(key, dims, pieces, least, high):
    gain = 1.0
    for axis_at, blocks in pieces:
        heights = jax.random.uniform(jax.random.fold_in(jax.random.fold_in(key, 6), axis_at), (blocks,), jnp.float32, least / len(pieces), high / len(pieces))
        gain = gain * jnp.repeat(jnp.exp(heights), dims[axis_at] // blocks).reshape((-1,) + (1,) * (len(dims) - 1 - axis_at))
    return gain


def gaussian(rng, extent, width, bound, cuts=(), kind=jnp.bfloat16):
    entries = width * jax.random.normal(rng, extent, jnp.float32)
    if cuts:
        entries = entries * levels(rng, extent, cuts, -0.22, 0.18)
    return jnp.clip(entries, -bound, bound).astype(kind)


def setup_inputs(seed: int = 0) -> dict:
    seeds = jax.random.split(jax.random.key(seed), 8)
    tile_values = jnp.clip(0.019897461 * jax.random.uniform(seeds[0], (N_ROW, N_COL * N_DEPTH, TMAX, TILE, TILE), jnp.float32) ** levels(seeds[0], (N_ROW, N_COL * N_DEPTH, TMAX, TILE, TILE), ((0, 8), (1, 64)), -0.2, 0.2), 0.0, 0.019897461).astype(jnp.bfloat16)
    tile_rows = draw_tile_rows(jax.random.fold_in(seeds[7], 71), 0)
    tile_cols = draw_tile_cols(jax.random.fold_in(seeds[7], 71), 0)
    tile_count = draw_tile_count(jax.random.fold_in(seeds[7], 71), 0)
    features = gaussian(seeds[4], (NODES, F), 1.0, 6.0, ((0, 64),))
    weight = gaussian(seeds[5], (F, HID), F ** -0.5, 0.5)
    cotangent = gaussian(seeds[6], (NODES, HID), 1.0, 6.0, ((0, 512),))
    return dict(tile_values=tile_values, tile_rows=tile_rows, tile_cols=tile_cols, tile_count=tile_count, features=features, weight=weight, cotangent=cotangent)


def silu_slope(pre):
    sig = jax.nn.sigmoid(pre)
    return sig * (1.0 + pre * (1.0 - sig))

def reference(tile_values, tile_rows, tile_cols, tile_count, features, weight, cotangent):
    inner_slabs = N_COL * N_DEPTH
    slots = jnp.arange(TMAX, dtype=jnp.int32)
    live = slots[None, None, :] < tile_count[:, :, None]
    row_target = jnp.where(live, tile_rows, RB).astype(jnp.int32)
    col_target = jnp.where(live, tile_cols, CB).astype(jnp.int32)
    blocks = features.reshape(inner_slabs, CB, TILE, F)

    def forward_slab(inputs):
        values, cols, targets = inputs

        def add_device(acc, device):
            tiles, picks, where_to, feats = device
            prod = jnp.einsum('tij,tjf->tif', tiles.astype(jnp.float32), feats[picks].astype(jnp.float32))
            return (acc + jax.ops.segment_sum(prod, where_to, num_segments=RB + 1), None)
        start = jnp.zeros((RB + 1, TILE, F), jnp.float32)
        acc, unused = lax.scan(add_device, start, (values, cols, targets, blocks))
        return acc[:RB]
    agg = lax.map(forward_slab, (tile_values, tile_cols, row_target))
    agg = agg.reshape(NODES, F).astype(jnp.bfloat16)
    pre = jnp.dot(agg, weight, preferred_element_type=jnp.float32)
    activations = jax.nn.silu(pre).astype(jnp.bfloat16)
    grad_pre = (cotangent.astype(jnp.float32) * silu_slope(pre)).astype(jnp.bfloat16)
    weight_grad = jnp.dot(agg.T, grad_pre, preferred_element_type=jnp.float32) / math.sqrt(NODES)
    grad_agg = jnp.dot(grad_pre, weight.T, preferred_element_type=jnp.float32).astype(jnp.bfloat16)
    grad_slabs = grad_agg.reshape(N_ROW, RB, TILE, F)

    def backward_slab(acc, inputs):
        values, rows, targets, grad_slab = inputs

        def one_device(device):
            tiles, picks, where_to = device
            prod = jnp.einsum('tij,tiw->tjw', tiles.astype(jnp.float32), grad_slab[picks].astype(jnp.float32))
            return jax.ops.segment_sum(prod, where_to, num_segments=CB + 1)[:CB]
        return (acc + lax.map(one_device, (values, rows, targets)), None)
    start = jnp.zeros((inner_slabs, CB, TILE, F), jnp.float32)
    inner, unused = lax.scan(backward_slab, start, (tile_values, tile_rows, col_target, grad_slabs))
    input_grad = inner.reshape(inner_slabs, CB * TILE, F).astype(jnp.bfloat16)
    return (activations, input_grad, weight_grad)
```

```python
import functools
import math

import jax
import jax.numpy as jnp
from jax import lax
from jax.experimental import pallas as pl
from jax.experimental.pallas import tpu as pltpu
from jax.sharding import PartitionSpec as P

TILE = 128
Z_HI = 2
CORES = 2
BF16 = jnp.bfloat16
F32 = jnp.float32


def kernel(
    sizes, table, vals_in, feat_in, w_in, cot_in, act_out, ig_out, wg_out,
    vals, valst, feat, w, cot, act, part, sb, rb, qs, own, slots, zsend, zrecv, g, acc,
    xs, xr, ig, wt, wr, wslots, wz, wsend, wrecv, wo,
    load_sem, out_sem, s1s, s1r, s2s, s2r, zsem, ga_s, ga_r, gp_r, gc_s, gc_r,
    xsem, w1, w2, w3, w4, w5, w6,
):
    n_row, n_y, n_x, ch, n_cb, block_tiles, slots_max = sizes
    n_blocks = Z_HI * n_y
    plane = n_x * n_y
    zc = n_cb * TILE // n_row
    row, col, depth = lax.axis_index("row"), lax.axis_index("col"), lax.axis_index("depth")
    zh, y = lax.div(col, n_y), lax.rem(col, n_y)
    x, core = lax.div(depth, CORES), lax.rem(depth, CORES)
    z_other, other = 1 - zh, 1 - core
    here = y * n_x + x

    sibling = (row, col, x * CORES + other)
    partner = (row, z_other * n_y + y, depth)

    def in_plane(dy, dx):
        yy, xx = lax.rem(y + dy, n_y), lax.rem(x + dx, n_x)
        return yy, xx, (row, zh * n_y + yy, xx * CORES + core)

    def in_row(dz):
        rr = lax.rem(row + dz, n_row)
        return rr, (rr, col, depth)

    offsets = [(dy, dx) for dy in range(n_y) for dx in range(n_x) if (dy, dx) != (0, 0)]

    def send(src, dst, send_sem, recv_sem, device):
        pltpu.make_async_remote_copy(
            src_ref=src, dst_ref=dst, send_sem=send_sem, recv_sem=recv_sem,
            device_id=device, device_id_type=pl.DeviceIdType.MESH,
        ).start()

    def wait(ref, sem):
        pltpu.make_async_copy(ref, ref, sem).wait()

    loads = [
        pltpu.make_async_copy(feat_in, feat, load_sem.at[0]),
        pltpu.make_async_copy(vals_in.at[0, 0], vals.at[pl.ds(0, slots_max)], load_sem.at[1]),
        pltpu.make_async_copy(w_in, w, load_sem.at[2]),
        pltpu.make_async_copy(cot_in, cot, load_sem.at[3]),
    ]
    for load in loads:
        load.start()

    barrier = pltpu.get_barrier_semaphore()
    peers = [sibling, partner]
    peers += [in_plane(dy, dx)[2] for dy, dx in offsets]
    peers += [in_row(dz)[1] for dz in range(1, n_row)]
    for peer in peers:
        pl.semaphore_signal(barrier, inc=1, device_id=peer, device_id_type=pl.DeviceIdType.MESH)

    vals[slots_max] = jnp.zeros((TILE, TILE), BF16)
    valst[slots_max] = jnp.zeros((TILE, TILE), BF16)
    loads[0].wait()
    loads[1].wait()
    pl.semaphore_wait(barrier, len(peers))

    def place(j):
        phase, dy = lax.div(j, n_y), lax.rem(j + 1, n_y)
        z = lax.rem(zh + 1 + phase, Z_HI)
        return phase, dy, z * n_y + lax.rem(y + dy, n_y)

    def chunk(b, xx, cc):
        return part[b, pl.ds(pl.multiple_of((xx * CORES + cc) * ch, 16), ch), :]

    def forward(j, carry):
        @pl.when(j < n_blocks)
        def _():
            _, _, b = place(j)
            for i in range(block_tiles):
                at = (b * block_tiles + i) * n_cb
                lhs = jnp.concatenate([vals[table[at + c]] for c in range(n_cb)], axis=1)
                part[b, i * TILE : (i + 1) * TILE, :] = jnp.dot(
                    lhs, feat[...], preferred_element_type=F32
                )
            for xx in range(n_x):
                sb[b, xx] = chunk(b, xx, other).astype(BF16)
            send(sb.at[b], rb.at[b], s1s, s1r.at[b], sibling)

        @pl.when(j > 0)
        def _():
            phase, dy, b = place(j - 1)
            wait(rb.at[b], s1r.at[b])
            for dx in range(n_x):
                yy, xx, device = in_plane(dy, dx)
                total = chunk(b, xx, core) + rb[b, xx].astype(F32)
                qs[b, xx] = total.astype(BF16)
                slot = dy * n_x + dx
                if dx == 0:

                    @pl.when(dy == 0)
                    def _():
                        own[phase] = total

                    @pl.when(dy != 0)
                    def _():
                        send(qs.at[b, xx], slots.at[phase, slot], s2s, s2r.at[phase], device)
                else:
                    send(qs.at[b, xx], slots.at[phase, slot], s2s, s2r.at[phase], device)

        return carry

    lax.fori_loop(0, n_blocks + 1, forward, 0)

    def plane_sum(phase):
        wait(slots.at[phase, pl.ds(1, plane - 1)], s2r.at[phase])
        return lax.fori_loop(
            1, plane, lambda k, t: t + slots[phase, k].astype(F32), own[phase]
        )

    zsend[...] = plane_sum(0).astype(BF16)
    send(zsend, zrecv, zsem.at[0], zsem.at[1], partner)

    def turn(t, carry):
        valst[t] = vals[t].T
        return carry

    lax.fori_loop(0, slots_max, turn, 0)
    total = plane_sum(1)
    loads[2].wait()
    loads[3].wait()
    wait(zrecv, zsem.at[1])
    agg = (total + zrecv[...].astype(F32)).astype(BF16)

    pre = jnp.dot(agg, w[...], preferred_element_type=F32)
    sig = jax.nn.sigmoid(pre)
    act[...] = (pre * sig).astype(BF16)
    slope = sig * (1.0 + pre * (1.0 - sig))
    grad_pre = (cot[...].astype(F32) * slope).astype(BF16)
    grad_agg = lax.dot_general(
        grad_pre, w[...], (((1,), (1,)), ((), ())), preferred_element_type=F32
    ).astype(BF16)
    g[col, x, core] = grad_agg

    b_here = z_other * n_y + y
    mine = g.at[col, x, core]
    send(mine, mine, ga_s, gp_r, partner)
    for dy, dx in offsets:
        send(mine, mine, ga_s, ga_r.at[0, dy], in_plane(dy, dx)[2])

    terms = lax.dot_general(agg, grad_pre, (((0,), (0,)), ((), ())), preferred_element_type=F32)
    wt[0] = terms[:, :TILE].reshape(wt.shape[1:])
    wt[1] = terms[:, TILE:].reshape(wt.shape[1:])
    send(wt.at[other], wr, w1.at[0], w1.at[1], sibling)
    act_copy = pltpu.make_async_copy(act, act_out, out_sem.at[0])
    act_copy.start()

    acc[...] = jnp.zeros_like(acc)

    def pass_on(phase, dy):
        z = lax.rem(zh + phase, Z_HI)
        b = z * n_y + lax.rem(y + n_y - dy, n_y)
        if dy == 0:
            wait(slots.at[0, pl.ds(0, n_x - 1)], ga_r.at[phase, dy])
        else:
            wait(g.at[b, pl.ds(0, n_x), core], ga_r.at[phase, dy])
        group = g.at[b, pl.ds(0, n_x), core]
        send(group, group, gc_s, gc_r.at[phase, dy], sibling)

    def backward(phase):
        def step(dy, carry):
            z = lax.rem(zh + phase, Z_HI)
            b = z * n_y + lax.rem(y + n_y - dy, n_y)
            wait(g.at[b, pl.ds(0, n_x), other], gc_r.at[phase, dy])
            grad = g[b].reshape(block_tiles * TILE, TILE)
            for c in range(n_cb):
                at = b * block_tiles * n_cb + c
                lhs = jnp.concatenate(
                    [valst[table[at + i * n_cb]] for i in range(block_tiles)], axis=1
                )
                acc[c * TILE : (c + 1) * TILE, :] += jnp.dot(
                    lhs, grad, preferred_element_type=F32
                )
            return carry

        lax.fori_loop(0, n_y, step, 0)

    wait(g.at[b_here, x, core], gp_r)
    theirs = g.at[b_here, x, core]
    for dy, dx in offsets:
        send(theirs, theirs, ga_s, ga_r.at[1, dy], in_plane(dy, dx)[2])
    wait(wr, w1.at[1])
    wt[core] = wt[core] + wr[...]
    for dy, dx in offsets:
        yy, xx, device = in_plane(dy, dx)
        send(wt.at[core, yy * n_x + xx], wslots.at[dy * n_x + dx], w2.at[0], w2.at[1], device)

    for dy in range(n_y):
        pass_on(0, dy)
    wait(wslots.at[pl.ds(1, plane - 1)], w2.at[1])
    wz[row] = lax.fori_loop(1, plane, lambda k, t: t + wslots[k], wt[core, here])
    for dz in range(1, n_row):
        send(wz.at[row], wz.at[row], w3.at[0], w3.at[1], in_row(dz)[1])

    backward(0)
    for dy in range(n_y):
        pass_on(1, dy)
    wait(wz.at[pl.ds(0, n_row - 1)], w3.at[1])
    wsend[...] = lax.fori_loop(1, n_row, lambda k, t: t + wz[k], wz[0])
    send(wsend, wrecv, w4.at[0], w4.at[1], partner)

    backward(1)
    for d in range(n_row):
        xs[d] = acc[d * zc : (d + 1) * zc, :].astype(BF16)
    for dz in range(1, n_row):
        rr, device = in_row(dz)
        send(xs.at[rr], xr.at[dz], xsem.at[0], xsem.at[1], device)

    scale = 1.0 / math.sqrt(n_row * n_blocks * block_tiles * TILE)
    wait(wrecv, w4.at[1])
    wo[core, here] = (wsend[...] + wrecv[...]) * scale
    final = wo.at[core, here]
    for dy, dx in offsets:
        send(final, final, w5.at[0], w5.at[1], in_plane(dy, dx)[2])
    wait(wo.at[core, pl.ds(0, plane - 1)], w5.at[1])
    send(wo.at[core], wo.at[core], w6.at[0], w6.at[1], sibling)

    inner = acc[pl.ds(pl.multiple_of(row * zc, 16), zc), :]
    wait(xr.at[pl.ds(1, n_row - 1)], xsem.at[1])
    ig[...] = lax.fori_loop(1, n_row, lambda k, t: t + xr[k].astype(F32), inner).astype(BF16)
    ig_copy = pltpu.make_async_copy(ig, ig_out, out_sem.at[1])
    ig_copy.start()
    wait(wo.at[other], w6.at[1])
    wg_copies = [
        pltpu.make_async_copy(wo.at[c], wg_out.at[c], out_sem.at[2 + c]) for c in range(CORES)
    ]
    for copy in wg_copies:
        copy.start()

    wait(sb, s1s)
    wait(slots.at[:, pl.ds(1, plane - 1)], s2s)
    wait(zsend, zsem.at[0])
    wait(slots.at[0], ga_s)
    wait(slots.at[0, pl.ds(1, plane - 1)], ga_s)
    wait(sb, gc_s)
    wait(wt.at[other], w1.at[0])
    wait(wslots.at[pl.ds(1, plane - 1)], w2.at[0])
    wait(wz.at[pl.ds(0, n_row - 1)], w3.at[0])
    wait(wsend, w4.at[0])
    wait(wo.at[core, pl.ds(0, plane - 1)], w5.at[0])
    wait(wo.at[core], w6.at[0])
    wait(xr.at[pl.ds(1, n_row - 1)], xsem.at[0])
    for copy in [act_copy, ig_copy] + wg_copies:
        copy.wait()


def local(tile_values, tile_rows, tile_cols, tile_count, features, weight, cotangent):
    n_row, n_col, n_depth = lax.axis_size("row"), lax.axis_size("col"), lax.axis_size("depth")
    n_y, n_x = n_col // Z_HI, n_depth // CORES
    ch, hid = cotangent.shape
    f = features.shape[1]
    n_cb = features.shape[0] // TILE
    n_blocks = n_col
    block_rows = n_depth * ch
    block_tiles = block_rows // TILE
    n_tiles = n_blocks * block_tiles
    slots_max = tile_values.shape[2]
    plane = n_x * n_y
    zc = features.shape[0] // n_row
    piece = f // plane

    slot = jnp.arange(slots_max, dtype=jnp.int32)
    key = jnp.where(slot < tile_count[0, 0], tile_rows[0, 0] * n_cb + tile_cols[0, 0], -1)
    where_at = jnp.arange(n_tiles * n_cb, dtype=jnp.int32)
    table = jnp.min(
        jnp.where(key[:, None] == where_at[None, :], slot[:, None], slots_max), axis=0
    )

    sizes = (n_row, n_y, n_x, ch, n_cb, block_tiles, slots_max)
    vmem, dma = pltpu.VMEM, pltpu.SemaphoreType.DMA
    anywhere = pl.BlockSpec(memory_space=pl.ANY)
    act, ig, wg = pl.pallas_call(
        functools.partial(kernel, sizes),
        out_shape=(
            jax.ShapeDtypeStruct((ch, hid), BF16),
            jax.ShapeDtypeStruct((zc, f), BF16),
            jax.ShapeDtypeStruct((CORES, plane, piece, TILE), F32),
        ),
        in_specs=[pl.BlockSpec(memory_space=pltpu.SMEM)] + [anywhere] * 4,
        out_specs=(anywhere,) * 3,
        scratch_shapes=[
            vmem((slots_max + 1, TILE, TILE), BF16),
            vmem((slots_max + 1, TILE, TILE), BF16),
            vmem(features.shape, BF16),
            vmem(weight.shape, BF16),
            vmem((ch, hid), BF16),
            vmem((ch, hid), BF16),
            vmem((n_blocks, block_rows, f), F32),
            vmem((n_blocks, n_x, ch, f), BF16),
            vmem((n_blocks, n_x, ch, f), BF16),
            vmem((n_blocks, n_x, ch, f), BF16),
            vmem((Z_HI, ch, f), F32),
            vmem((Z_HI, plane, ch, f), BF16),
            vmem((ch, f), BF16),
            vmem((ch, f), BF16),
            vmem((n_blocks, n_x, CORES, ch, f), BF16),
            vmem((n_cb * TILE, f), F32),
            vmem((n_row, zc, f), BF16),
            vmem((n_row, zc, f), BF16),
            vmem((zc, f), BF16),
            vmem((CORES, plane, piece, TILE), F32),
            vmem((plane, piece, TILE), F32),
            vmem((plane, piece, TILE), F32),
            vmem((n_row, piece, TILE), F32),
            vmem((piece, TILE), F32),
            vmem((piece, TILE), F32),
            vmem((CORES, plane, piece, TILE), F32),
            dma((4,)),
            dma((4,)),
            dma,
            dma((n_blocks,)),
            dma,
            dma((Z_HI,)),
            dma((2,)),
            dma,
            dma((Z_HI, n_y)),
            dma,
            dma,
            dma((Z_HI, n_y)),
            dma((2,)),
            dma((2,)),
            dma((2,)),
            dma((2,)),
            dma((2,)),
            dma((2,)),
            dma((2,)),
        ],
        compiler_params=pltpu.CompilerParams(
            collective_id=0, has_side_effects=True, vmem_limit_bytes=40 * 1024 * 1024
        ),
        name="graph_layer",
    )(table, tile_values, features, weight, cotangent)
    weight_grad = wg.reshape(CORES, f, TILE).transpose(1, 0, 2).reshape(f, hid)
    return act, ig[None], weight_grad


def solution(mesh):
    in_specs = (
        P("row", ("col", "depth"), None, None, None),
        P("row", ("col", "depth"), None),
        P("row", ("col", "depth"), None),
        P("row", ("col", "depth")),
        P(("col", "depth"), None),
        P(),
        P(("row", "col", "depth"), None),
    )
    out_specs = (P(("row", "col", "depth"), None), P(("col", "depth"), "row", None), P())
    return jax.shard_map(local, mesh=mesh, in_specs=in_specs, out_specs=out_specs, check_vma=False)
```

```python
import functools
import math

import jax
import jax.numpy as jnp
from jax import lax
from jax.experimental import pallas as pl
from jax.experimental.pallas import tpu as pltpu
from jax.sharding import PartitionSpec as P

TILE = 128
Z_HI = 2
CORES = 2
BF16 = jnp.bfloat16
F32 = jnp.float32


def kernel(
    sizes, table, cols, vals_in, feat_in, w_in, cot_in, act_out, ig_out, wg_out,
    vals, valst, feat, w, cot, act, dense, prod, part, sb, rb, qs, own, slots, zsend, zrecv, g, acc,
    xs, xr, ig, wt, wr, wslots, wz, wo,
    load_sem, out_sem, csem, s1s, s1r, s2s, s2r, zs, zr, ga_s, ga_r, gc_s, gc_r,
    xsem, w1, w2, w3, w5, w6,
):
    n_row, n_y, n_x, ch, n_cb, block_tiles, slots_max = sizes
    n_blocks = Z_HI * n_y
    plane = n_x * n_y
    zc = n_cb * TILE // n_row
    row, col, depth = lax.axis_index("row"), lax.axis_index("col"), lax.axis_index("depth")
    zh, y = lax.div(col, n_y), lax.rem(col, n_y)
    x, core = lax.div(depth, CORES), lax.rem(depth, CORES)
    z_other, other = 1 - zh, 1 - core
    here = y * n_x + x

    sibling = (row, col, x * CORES + other)
    partner = (row, z_other * n_y + y, depth)

    def in_plane(dy, dx):
        yy, xx = lax.rem(y + dy, n_y), lax.rem(x + dx, n_x)
        return yy, xx, (row, zh * n_y + yy, xx * CORES + core)

    def in_row(dz):
        rr = lax.rem(row + dz, n_row)
        return rr, (rr, col, depth)

    offsets = [(dy, dx) for dy in range(n_y) for dx in range(n_x) if (dy, dx) != (0, 0)]
    hops = lambda o: (min(o[0], n_y - o[0]), min(o[1], n_x - o[1]))
    offsets.sort(key=lambda o: (-sum(hops(o)), abs(hops(o)[0] - hops(o)[1]), o[0] + o[1]))
    first = ch // 32 * 16 + ch // 16 % 2 * 16
    pieces = [pl.ds(0, first), pl.ds(first, ch - first)]
    units = [(phase, half) for phase in range(Z_HI) for half in range(2)]
    strides = sorted(range(1, n_row), key=lambda dz: -abs(2 * dz - n_row))

    def send(src, dst, send_sem, recv_sem, device):
        pltpu.make_async_remote_copy(
            src_ref=src, dst_ref=dst, send_sem=send_sem, recv_sem=recv_sem,
            device_id=device, device_id_type=pl.DeviceIdType.MESH,
        ).start()

    def wait(ref, sem):
        pltpu.make_async_copy(ref, ref, sem).wait()

    barrier = pltpu.get_barrier_semaphore()
    peers = [sibling, partner]
    peers += [in_plane(dy, dx)[2] for dy, dx in offsets]
    peers += [in_row(dz)[1] for dz in strides]
    for peer in peers:
        pl.semaphore_signal(barrier, inc=1, device_id=peer, device_id_type=pl.DeviceIdType.MESH)

    quarter = slots_max // 4
    loads = [pltpu.make_async_copy(feat_in, feat, load_sem.at[0])]
    for q in range(4):
        span = pl.ds(q * quarter, quarter)
        loads.append(pltpu.make_async_copy(vals_in.at[0, 0, span], vals.at[span], load_sem.at[1 + q]))
    late_loads = [
        pltpu.make_async_copy(cot_in, cot.at[zh], load_sem.at[5]),
        pltpu.make_async_copy(w_in, w, load_sem.at[6]),
    ]
    for load in loads + late_loads:
        load.start()

    valst[slots_max] = jnp.zeros((TILE, TILE), BF16)
    prod[slots_max] = jnp.zeros((TILE, TILE), F32)
    for load in loads:
        load.wait()

    def multiply(t, carry):
        for u in range(4):
            s = 4 * t + u
            prod[s] = jnp.dot(vals[s], feat[cols[s]], preferred_element_type=F32)
        return carry

    lax.fori_loop(0, slots_max // 4, multiply, 0)

    def chunk(b, xx, cc):
        return part[b, pl.ds(pl.multiple_of((xx * CORES + cc) * ch, 16), ch), :]

    def gather_products(b, carry):
        for i in range(block_tiles):
            at = (b * block_tiles + i) * n_cb
            total = prod[table[at]]
            for c in range(1, n_cb):
                total = total + prod[table[at + c]]
            part[b, i * TILE : (i + 1) * TILE, :] = total
        for xx in range(n_x):
            sb[b, xx] = chunk(b, xx, other).astype(BF16)
        return carry

    lax.fori_loop(0, n_blocks, gather_products, 0)
    pl.semaphore_wait(barrier, len(peers))
    for b in range(n_blocks):
        send(sb.at[b], rb.at[b], s1s, s1r.at[b], sibling)
    for load in late_loads:
        load.wait()
    send(cot.at[zh], cot.at[zh], csem.at[0], csem.at[1], partner)

    for phase in range(Z_HI):

        def pair(yy, carry):
            b = phase * n_y + yy
            wait(rb.at[b], s1r.at[b])
            for xx in range(n_x):
                qs[b, xx] = (chunk(b, xx, core) + rb[b, xx].astype(F32)).astype(BF16)
            return carry

        lax.fori_loop(0, n_y, pair, 0)
        for half, rows in enumerate(pieces):
            for dy, dx in offsets:
                yy, xx, device = in_plane(dy, dx)
                send(
                    qs.at[phase * n_y + yy, xx, rows], slots.at[phase, dy * n_x + dx, rows],
                    s2s, s2r.at[phase, half], device,
                )
        b = phase * n_y + y
        own[phase] = chunk(b, x, core) + rb[b, x].astype(F32)

    for phase, half in units:
        rows = pieces[half]
        wait(slots.at[phase, pl.ds(1, plane - 1), rows], s2r.at[phase, half])
        total = own[phase, rows]
        for k in range(1, plane):
            total = total + slots[phase, k, rows].astype(F32)
        zsend[phase, rows] = total.astype(BF16)
        mine = zsend.at[phase, rows]
        send(mine, zrecv.at[phase, rows], zs, zr.at[phase, half], partner)

    def turn(t, carry):
        valst[t] = vals[t].T
        return carry

    lax.fori_loop(0, slots_max, turn, 0)
    wait(cot.at[z_other], csem.at[1])

    for phase, half in units:
        rows = pieces[half]
        wait(zrecv.at[phase, rows], zr.at[phase, half])
        agg = (zsend[phase, rows].astype(F32) + zrecv[phase, rows].astype(F32)).astype(BF16)
        pre = jnp.dot(agg, w[...], preferred_element_type=F32)
        sig = jax.nn.sigmoid(pre)
        slope = sig * (1.0 + pre * (1.0 - sig))
        grad_pre = (cot[phase, rows].astype(F32) * slope).astype(BF16)
        grad_agg = lax.dot_general(
            grad_pre, w[...], (((1,), (1,)), ((), ())), preferred_element_type=F32
        )
        mine = g.at[phase * n_y + y, x, core, rows]
        mine[...] = grad_agg.astype(BF16)
        for dy, dx in offsets:
            send(mine, mine, ga_s, ga_r.at[phase, half, dy], in_plane(dy, dx)[2])
        act[phase, rows] = (pre * sig).astype(BF16)
        terms = lax.dot_general(
            agg, grad_pre, (((0,), (0,)), ((), ())), preferred_element_type=F32
        )
        for lane in range(CORES):
            term = terms[:, lane * TILE : (lane + 1) * TILE].reshape(wt.shape[1:])
            wt[lane] = term if (phase, half) == (0, 0) else wt[lane] + term
    send(wt.at[other], wr, w1.at[0], w1.at[1], sibling)
    act_copy = pltpu.make_async_copy(act.at[zh], act_out, out_sem.at[0])
    act_copy.start()

    wait(wr, w1.at[1])
    wt[core] = wt[core] + wr[...]
    for dy, dx in offsets:
        yy, xx, device = in_plane(dy, dx)
        send(wt.at[core, yy * n_x + xx], wslots.at[dy * n_x + dx], w2.at[0], w2.at[1], device)

    acc[...] = jnp.zeros_like(acc)

    def gather(phase):
        def source(i):
            dy = i + lax.div(i, 2) * (5 - 2 * i)
            return dy, phase * n_y + lax.rem(y + n_y - dy, n_y)

        def step(i, carry):
            @pl.when(i < n_y)
            def _():
                dy, b = source(i)
                group = g.at[b, pl.ds(0, n_x), core]

                for half, rows in enumerate(pieces):

                    @pl.when(dy == 0)
                    def _():
                        wait(slots.at[0, pl.ds(0, n_x - 1), rows], ga_r.at[phase, half, dy])

                    @pl.when(dy != 0)
                    def _():
                        wait(g.at[b, pl.ds(0, n_x), core, rows], ga_r.at[phase, half, dy])

                send(group, group, gc_s, gc_r.at[phase, dy], sibling)

            @pl.when(i > 0)
            def _():
                dy, b = source(i - 1)
                wait(g.at[b, pl.ds(0, n_x), other], gc_r.at[phase, dy])
                for c in range(n_cb):
                    for t in range(block_tiles):
                        slot = table[(b * block_tiles + t) * n_cb + c]
                        dense[c * TILE : (c + 1) * TILE, t * TILE : (t + 1) * TILE] = valst[slot]
                grad = g[b].reshape(block_tiles * TILE, TILE)
                acc[...] += jnp.dot(dense[...], grad, preferred_element_type=F32)

            return carry

        lax.fori_loop(0, n_y + 1, step, 0)

    gather(0)
    wait(wslots.at[pl.ds(1, plane - 1)], w2.at[1])
    piece = wt[core, here]
    for k in range(1, plane):
        piece = piece + wslots[k]
    wz[row] = piece
    for dz in strides:
        send(wz.at[row], wz.at[row], w3.at[0], w3.at[1], in_row(dz)[1])

    gather(1)
    for d in range(n_row):
        xs[d] = acc[d * zc : (d + 1) * zc, :].astype(BF16)
    for dz in strides:
        rr, device = in_row(dz)
        send(xs.at[rr], xr.at[dz], xsem.at[0], xsem.at[1], device)

    wait(wz.at[pl.ds(0, n_row - 1)], w3.at[1])
    piece = wz[0]
    for k in range(1, n_row):
        piece = piece + wz[k]
    scale = 1.0 / math.sqrt(n_row * n_blocks * block_tiles * TILE)
    final = wo.at[core, here]
    final[...] = piece * scale
    for dy, dx in offsets:
        send(final, final, w5.at[0], w5.at[1], in_plane(dy, dx)[2])
    wait(wo.at[core, pl.ds(0, plane - 1)], w5.at[1])
    send(wo.at[core], wo.at[core], w6.at[0], w6.at[1], sibling)

    total = acc[pl.ds(pl.multiple_of(row * zc, 16), zc), :]
    wait(xr.at[pl.ds(1, n_row - 1)], xsem.at[1])
    for k in range(1, n_row):
        total = total + xr[k].astype(F32)
    ig[...] = total.astype(BF16)
    ig_copy = pltpu.make_async_copy(ig, ig_out, out_sem.at[1])
    ig_copy.start()
    wait(wo.at[other], w6.at[1])
    wg_copies = [
        pltpu.make_async_copy(wo.at[c], wg_out.at[c], out_sem.at[2 + c]) for c in range(CORES)
    ]
    for copy in wg_copies:
        copy.start()

    wait(sb, s1s)
    wait(cot.at[zh], csem.at[0])
    wait(slots.at[:, pl.ds(1, plane - 1)], s2s)
    wait(zsend, zs)
    wait(slots.at[:, pl.ds(1, plane - 1)], ga_s)
    wait(sb, gc_s)
    wait(wt.at[other], w1.at[0])
    wait(wslots.at[pl.ds(1, plane - 1)], w2.at[0])
    wait(wz.at[pl.ds(0, n_row - 1)], w3.at[0])
    wait(wo.at[core, pl.ds(0, plane - 1)], w5.at[0])
    wait(wo.at[core], w6.at[0])
    wait(xr.at[pl.ds(1, n_row - 1)], xsem.at[0])
    for copy in [act_copy, ig_copy] + wg_copies:
        copy.wait()


def local(tile_values, tile_rows, tile_cols, tile_count, features, weight, cotangent):
    n_row, n_col, n_depth = lax.axis_size("row"), lax.axis_size("col"), lax.axis_size("depth")
    n_y, n_x = n_col // Z_HI, n_depth // CORES
    ch, hid = cotangent.shape
    f = features.shape[1]
    n_cb = features.shape[0] // TILE
    n_blocks = n_col
    block_rows = n_depth * ch
    block_tiles = block_rows // TILE
    n_tiles = n_blocks * block_tiles
    slots_max = tile_values.shape[2]
    plane = n_x * n_y
    zc = features.shape[0] // n_row
    piece = f // plane

    slot = jnp.arange(slots_max, dtype=jnp.int32)
    key = jnp.where(slot < tile_count[0, 0], tile_rows[0, 0] * n_cb + tile_cols[0, 0], -1)
    where_at = jnp.arange(n_tiles * n_cb, dtype=jnp.int32)
    table = jnp.min(
        jnp.where(key[:, None] == where_at[None, :], slot[:, None], slots_max), axis=0
    )

    sizes = (n_row, n_y, n_x, ch, n_cb, block_tiles, slots_max)
    vmem, dma = pltpu.VMEM, pltpu.SemaphoreType.DMA
    operands = [
        pltpu.with_memory_space_constraint(a, pltpu.HBM)
        for a in (tile_values, features.reshape(n_cb, TILE, f), weight, cotangent)
    ]
    anywhere = pl.BlockSpec(memory_space=pl.ANY)
    act, ig, wg = pl.pallas_call(
        functools.partial(kernel, sizes),
        out_shape=(
            vmem((ch, hid), BF16),
            vmem((zc, f), BF16),
            vmem((CORES, plane, piece, TILE), F32),
        ),
        in_specs=[pl.BlockSpec(memory_space=pltpu.SMEM)] * 2
        + [pl.BlockSpec(memory_space=pltpu.HBM)] * 4,
        out_specs=(anywhere,) * 3,
        scratch_shapes=[
            vmem((slots_max, TILE, TILE), BF16),
            vmem((slots_max + 1, TILE, TILE), BF16),
            vmem((n_cb, TILE, f), BF16),
            vmem(weight.shape, BF16),
            vmem((Z_HI, ch, hid), BF16),
            vmem((Z_HI, ch, hid), BF16),
            vmem((n_cb * TILE, n_cb * TILE), BF16),
            vmem((slots_max + 1, TILE, f), F32),
            vmem((n_blocks, block_rows, f), F32),
            vmem((n_blocks, n_x, ch, f), BF16),
            vmem((n_blocks, n_x, ch, f), BF16),
            vmem((n_blocks, n_x, ch, f), BF16),
            vmem((Z_HI, ch, f), F32),
            vmem((Z_HI, plane, ch, f), BF16),
            vmem((Z_HI, ch, f), BF16),
            vmem((Z_HI, ch, f), BF16),
            vmem((n_blocks, n_x, CORES, ch, f), BF16),
            vmem((n_cb * TILE, f), F32),
            vmem((n_row, zc, f), BF16),
            vmem((n_row, zc, f), BF16),
            vmem((zc, f), BF16),
            vmem((CORES, plane, piece, TILE), F32),
            vmem((plane, piece, TILE), F32),
            vmem((plane, piece, TILE), F32),
            vmem((n_row, piece, TILE), F32),
            vmem((CORES, plane, piece, TILE), F32),
            dma((7,)),
            dma((4,)),
            dma((2,)),
            dma,
            dma((n_blocks,)),
            dma,
            dma((Z_HI, 2)),
            dma,
            dma((Z_HI, 2)),
            dma,
            dma((Z_HI, 2, n_y)),
            dma,
            dma((Z_HI, n_y)),
            dma((2,)),
            dma((2,)),
            dma((2,)),
            dma((2,)),
            dma((2,)),
            dma((2,)),
        ],
        compiler_params=pltpu.CompilerParams(
            collective_id=0, has_side_effects=True, vmem_limit_bytes=40 * 1024 * 1024
        ),
        name="graph_layer",
    )(table, tile_cols[0, 0], *operands)
    weight_grad = wg.reshape(CORES, f, TILE).transpose(1, 0, 2).reshape(f, hid)
    return act, ig[None], weight_grad


def solution(mesh):
    in_specs = (
        P("row", ("col", "depth"), None, None, None),
        P("row", ("col", "depth"), None),
        P("row", ("col", "depth"), None),
        P("row", ("col", "depth")),
        P(("col", "depth"), None),
        P(),
        P(("row", "col", "depth"), None),
    )
    out_specs = (P(("row", "col", "depth"), None), P(("col", "depth"), "row", None), P())
    return jax.shard_map(local, mesh=mesh, in_specs=in_specs, out_specs=out_specs, check_vma=False)
```

```python
import functools
import math

import jax
import jax.numpy as jnp
from jax import lax
from jax.experimental import pallas as pl
from jax.experimental.pallas import tpu as pltpu
from jax.sharding import PartitionSpec as P

TILE = 128
Z_HI = 2
LOADS = 8
CORES = 2
BF16 = jnp.bfloat16
F32 = jnp.float32


def kernel(
    sizes, count_s, rows_in, cols_in, vals_in, feat_in, w_in, cot_in, act_out, ig_out, wg_out,
    rows_s, cols_s, places, table, vals, valst, feat, w, cot, act, dense, prod, part, sb, rb, qs, own, slots, zsend, zrecv, g, acc,
    xs, xr, wt, wr, wslots, wz, wo,
    slot_sem, table_sem, load_sem, csem, s1s, s1r, s2s, s2r, zs, zr, ga_s, ga_r, gc_s, gc_r,
    xsem, w1, w2, w3, w5, w6,
):
    n_row, n_y, n_x, ch, n_cb, block_tiles, slots_max = sizes
    n_blocks = Z_HI * n_y
    plane = n_x * n_y
    zc = n_cb * TILE // n_row
    row, col, depth = lax.axis_index("row"), lax.axis_index("col"), lax.axis_index("depth")
    zh, y = lax.div(col, n_y), lax.rem(col, n_y)
    x, core = lax.div(depth, CORES), lax.rem(depth, CORES)
    z_other, other = 1 - zh, 1 - core
    here = y * n_x + x

    sibling = (row, col, x * CORES + other)
    partner = (row, z_other * n_y + y, depth)

    def in_plane(dy, dx):
        yy, xx = lax.rem(y + dy, n_y), lax.rem(x + dx, n_x)
        return yy, xx, (row, zh * n_y + yy, xx * CORES + core)

    def in_row(dz):
        rr = lax.rem(row + dz, n_row)
        return rr, (rr, col, depth)

    offsets = [(dy, dx) for dy in range(n_y) for dx in range(n_x) if (dy, dx) != (0, 0)]
    hops = lambda o: (min(o[0], n_y - o[0]), min(o[1], n_x - o[1]))
    offsets.sort(key=lambda o: (-sum(hops(o)), abs(hops(o)[0] - hops(o)[1]), o[0] + o[1]))
    long = (ch // 16 + 1) // 2 * 16
    short = ch - long
    pieces = [
        [pl.ds(0, short), pl.ds(short, long)],
        [pl.ds(0, long), pl.ds(long, short)],
    ]
    units = [(phase, half) for phase in range(Z_HI) for half in range(2)]
    strides = sorted(range(1, n_row), key=lambda dz: -abs(2 * dz - n_row))

    def send(src, dst, send_sem, recv_sem, device):
        pltpu.make_async_remote_copy(
            src_ref=src, dst_ref=dst, send_sem=send_sem, recv_sem=recv_sem,
            device_id=device, device_id_type=pl.DeviceIdType.MESH,
        ).start()

    def wait(ref, sem):
        pltpu.make_async_copy(ref, ref, sem).wait()

    slot_loads = [
        pltpu.make_async_copy(rows_in, rows_s, slot_sem.at[0]),
        pltpu.make_async_copy(cols_in, cols_s, slot_sem.at[1]),
    ]
    part_slots = slots_max // LOADS
    value_loads = []
    for q in range(LOADS):
        span = pl.ds(q * part_slots, part_slots)
        value_loads.append(
            pltpu.make_async_copy(vals_in.at[0, 0, span], vals.at[span], load_sem.at[q])
        )
    feat_load = pltpu.make_async_copy(feat_in, feat, load_sem.at[LOADS])
    late_loads = [
        pltpu.make_async_copy(cot_in, cot.at[zh], load_sem.at[LOADS + 1]),
        pltpu.make_async_copy(w_in, w, load_sem.at[LOADS + 2]),
    ]
    for load in slot_loads + [feat_load] + value_loads + late_loads:
        load.start()

    barrier = pltpu.get_barrier_semaphore()
    peers = [sibling, partner]
    peers += [in_plane(dy, dx)[2] for dy, dx in offsets]
    peers += [in_row(dz)[1] for dz in strides]
    for peer in peers:
        pl.semaphore_signal(barrier, inc=1, device_id=peer, device_id_type=pl.DeviceIdType.MESH)

    valst[slots_max] = jnp.zeros((TILE, TILE), BF16)
    prod[slots_max] = jnp.zeros((TILE, TILE), F32)

    for load in slot_loads:
        load.wait()
    count = count_s[0, 0]
    place = lax.broadcasted_iota(jnp.int32, places.shape, 0) * TILE
    place = place + lax.broadcasted_iota(jnp.int32, places.shape, 1)

    def fill(t, found):
        for u in range(LOADS):
            s = t * LOADS + u
            key = jnp.where(s < count, rows_s[0, 0, s] * n_cb + cols_s[0, 0, s], -1)
            found = jnp.where(place == key, s, found)
        return found

    places[...] = lax.fori_loop(
        0, slots_max // LOADS, fill, jnp.full(places.shape, slots_max, jnp.int32)
    )
    table_copy = pltpu.make_async_copy(places, table, table_sem)
    table_copy.start()

    def slot_at(p):
        return table[lax.div(p, TILE), lax.rem(p, TILE)]

    feat_load.wait()

    for q in range(LOADS):
        value_loads[q].wait()

        def multiply(t, carry):
            for u in range(4):
                s = q * part_slots + 4 * t + u
                prod[s] = jnp.dot(vals[s], feat[cols_s[0, 0, s]], preferred_element_type=F32)
            return carry

        lax.fori_loop(0, part_slots // 4, multiply, 0)
    table_copy.wait()

    def chunk(b, xx, cc):
        return part[b, pl.ds(pl.multiple_of((xx * CORES + cc) * ch, 16), ch), :]

    def gather_products(j, carry):
        b = lax.div(j, n_y) * n_y + lax.rem(y + j, n_y)
        for i in range(block_tiles):
            at = (b * block_tiles + i) * n_cb
            total = prod[slot_at(at)]
            for c in range(1, n_cb):
                total = total + prod[slot_at(at + c)]
            part[b, i * TILE : (i + 1) * TILE, :] = total
        for xx in range(n_x):
            sb[b, xx] = chunk(b, xx, other).astype(BF16)
        send(sb.at[b], rb.at[b], s1s, s1r.at[b], sibling)
        return carry

    pl.semaphore_wait(barrier, len(peers))
    lax.fori_loop(0, n_blocks, gather_products, 0)
    for load in late_loads:
        load.wait()
    send(cot.at[zh], cot.at[zh], csem.at[0], csem.at[1], partner)

    for phase in range(Z_HI):

        def pair(i, carry):
            b = phase * n_y + lax.rem(y + i, n_y)
            wait(rb.at[b], s1r.at[b])
            for xx in range(n_x):
                qs[b, xx] = (chunk(b, xx, core) + rb[b, xx].astype(F32)).astype(BF16)
            return carry

        lax.fori_loop(0, n_y, pair, 0)
        for half, rows in enumerate(pieces[phase]):
            for dy, dx in offsets:
                yy, xx, device = in_plane(dy, dx)
                send(
                    qs.at[phase * n_y + yy, xx, rows], slots.at[phase, dy * n_x + dx, rows],
                    s2s, s2r.at[phase, half], device,
                )
        b = phase * n_y + y
        own[phase] = chunk(b, x, core) + rb[b, x].astype(F32)

    for phase, half in units:
        rows = pieces[phase][half]
        wait(slots.at[phase, pl.ds(1, plane - 1), rows], s2r.at[phase, half])
        total = own[phase, rows]
        for k in range(1, plane):
            total = total + slots[phase, k, rows].astype(F32)
        zsend[phase, rows] = total.astype(BF16)
        mine = zsend.at[phase, rows]
        send(mine, zrecv.at[phase, rows], zs, zr.at[phase, half], partner)

    def turn(t, carry):
        valst[t] = vals[t].T
        return carry

    lax.fori_loop(0, slots_max, turn, 0)
    wait(cot.at[z_other], csem.at[1])

    for phase, half in units:
        rows = pieces[phase][half]
        wait(zrecv.at[phase, rows], zr.at[phase, half])
        agg = (zsend[phase, rows].astype(F32) + zrecv[phase, rows].astype(F32)).astype(BF16)
        pre = jnp.dot(agg, w[...], preferred_element_type=F32)
        sig = jax.nn.sigmoid(pre)
        slope = sig * (1.0 + pre * (1.0 - sig))
        grad_pre = (cot[phase, rows].astype(F32) * slope).astype(BF16)
        grad_agg = lax.dot_general(
            grad_pre, w[...], (((1,), (1,)), ((), ())), preferred_element_type=F32
        )
        mine = g.at[phase * n_y + y, x, core, rows]
        mine[...] = grad_agg.astype(BF16)
        if (phase, half) != units[-1]:
            for dy, dx in offsets:
                send(mine, mine, ga_s, ga_r.at[phase, half, dy], in_plane(dy, dx)[2])
        terms = lax.dot_general(
            agg, grad_pre, (((0,), (0,)), ((), ())), preferred_element_type=F32
        )
        for lane in range(CORES):
            term = terms[:, lane * TILE : (lane + 1) * TILE].reshape(wt.shape[1:])
            wt[lane] = term if (phase, half) == units[0] else wt[lane] + term
        act[phase, rows] = (pre * sig).astype(BF16)

    send(wt.at[other], wr, w1.at[0], w1.at[1], sibling)
    act_out[...] = act[zh]
    wait(wr, w1.at[1])
    wt[core] = wt[core] + wr[...]
    for dy, dx in offsets:
        yy, xx, device = in_plane(dy, dx)
        send(wt.at[core, yy * n_x + xx], wslots.at[dy * n_x + dx], w2.at[0], w2.at[1], device)
    for dy, dx in offsets:
        send(mine, mine, ga_s, ga_r.at[phase, half, dy], in_plane(dy, dx)[2])

    acc[...] = jnp.zeros_like(acc)

    def gather(phase):
        def source(i):
            dy = i + lax.div(i, 2) * (5 - 2 * i)
            return dy, phase * n_y + lax.rem(y + n_y - dy, n_y)

        def step(i, carry):
            @pl.when(i < n_y)
            def _():
                dy, b = source(i)
                group = g.at[b, pl.ds(0, n_x), core]

                for half, rows in enumerate(pieces[phase]):

                    @pl.when(dy == 0)
                    def _():
                        wait(slots.at[0, pl.ds(0, n_x - 1), rows], ga_r.at[phase, half, dy])

                    @pl.when(dy != 0)
                    def _():
                        wait(g.at[b, pl.ds(0, n_x), core, rows], ga_r.at[phase, half, dy])

                send(group, group, gc_s, gc_r.at[phase, dy], sibling)

            @pl.when(i > 0)
            def _():
                dy, b = source(i - 1)
                wait(g.at[b, pl.ds(0, n_x), other], gc_r.at[phase, dy])
                for c in range(n_cb):
                    for t in range(block_tiles):
                        slot = slot_at((b * block_tiles + t) * n_cb + c)
                        dense[c * TILE : (c + 1) * TILE, t * TILE : (t + 1) * TILE] = valst[slot]
                grad = g[b].reshape(block_tiles * TILE, TILE)
                acc[...] += jnp.dot(dense[...], grad, preferred_element_type=F32)

            return carry

        lax.fori_loop(0, n_y + 1, step, 0)

    gather(0)
    wait(wslots.at[pl.ds(1, plane - 1)], w2.at[1])
    piece = wt[core, here]
    for k in range(1, plane):
        piece = piece + wslots[k]
    wz[row] = piece
    for dz in strides:
        send(wz.at[row], wz.at[row], w3.at[0], w3.at[1], in_row(dz)[1])

    gather(1)
    for d in range(n_row):
        xs[d] = acc[d * zc : (d + 1) * zc, :].astype(BF16)
    for dz in strides:
        rr, device = in_row(dz)
        send(xs.at[rr], xr.at[dz], xsem.at[0], xsem.at[1], device)

    wait(wz.at[pl.ds(0, n_row - 1)], w3.at[1])
    piece = wz[0]
    for k in range(1, n_row):
        piece = piece + wz[k]
    scale = 1.0 / math.sqrt(n_row * n_blocks * block_tiles * TILE)
    final = wo.at[core, here]
    final[...] = piece * scale
    for dy, dx in offsets:
        send(final, final, w5.at[0], w5.at[1], in_plane(dy, dx)[2])
    wait(wo.at[core, pl.ds(0, plane - 1)], w5.at[1])
    send(wo.at[core], wo.at[core], w6.at[0], w6.at[1], sibling)

    total = acc[pl.ds(pl.multiple_of(row * zc, 16), zc), :]
    wait(xr.at[pl.ds(1, n_row - 1)], xsem.at[1])
    for k in range(1, n_row):
        total = total + xr[k].astype(F32)
    ig_out[...] = total.astype(BF16)
    wait(wo.at[other], w6.at[1])
    for c in range(CORES):
        wg_out[c] = wo[c].reshape(TILE, TILE)

    wait(sb, s1s)
    wait(cot.at[zh], csem.at[0])
    wait(slots.at[:, pl.ds(1, plane - 1)], s2s)
    wait(zsend, zs)
    wait(slots.at[:, pl.ds(1, plane - 1)], ga_s)
    wait(sb, gc_s)
    wait(wt.at[other], w1.at[0])
    wait(wslots.at[pl.ds(1, plane - 1)], w2.at[0])
    wait(wz.at[pl.ds(0, n_row - 1)], w3.at[0])
    wait(wo.at[core, pl.ds(0, plane - 1)], w5.at[0])
    wait(wo.at[core], w6.at[0])
    wait(xr.at[pl.ds(1, n_row - 1)], xsem.at[0])


def deliver(act, ig, wg, act_out, ig_out, wg_out, sem):
    copies = [
        pltpu.make_async_copy(act, act_out, sem.at[0]),
        pltpu.make_async_copy(ig, ig_out, sem.at[1]),
    ]
    for c in range(CORES):
        lanes = pl.ds(c * TILE, TILE)
        copies.append(pltpu.make_async_copy(wg.at[c], wg_out.at[:, lanes], sem.at[2 + c]))
    for copy in copies:
        copy.start()
    for copy in copies:
        copy.wait()


def local(tile_values, tile_rows, tile_cols, tile_count, features, weight, cotangent):
    n_row, n_col, n_depth = lax.axis_size("row"), lax.axis_size("col"), lax.axis_size("depth")
    n_y, n_x = n_col // Z_HI, n_depth // CORES
    ch, hid = cotangent.shape
    f = features.shape[1]
    n_cb = features.shape[0] // TILE
    n_blocks = n_col
    block_rows = n_depth * ch
    block_tiles = block_rows // TILE
    slots_max = tile_values.shape[2]
    plane = n_x * n_y
    zc = features.shape[0] // n_row
    piece = f // plane

    sizes = (n_row, n_y, n_x, ch, n_cb, block_tiles, slots_max)
    vmem, dma = pltpu.VMEM, pltpu.SemaphoreType.DMA
    operands = [
        pltpu.with_memory_space_constraint(a, pltpu.HBM)
        for a in (
            tile_rows, tile_cols, tile_values, features.reshape(n_cb, TILE, f),
            weight, cotangent,
        )
    ]
    anywhere = pl.BlockSpec(memory_space=pl.ANY)
    act, ig, wg = pl.pallas_call(
        functools.partial(kernel, sizes),
        out_shape=(
            vmem((ch, hid), BF16),
            vmem((zc, f), BF16),
            vmem((CORES, f, TILE), F32),
        ),
        in_specs=[pl.BlockSpec(memory_space=pltpu.SMEM)]
        + [pl.BlockSpec(memory_space=pltpu.HBM)] * 6,
        out_specs=(pl.BlockSpec(memory_space=pltpu.VMEM),) * 3,
        scratch_shapes=[
            pltpu.SMEM(tile_rows.shape, jnp.int32),
            pltpu.SMEM(tile_cols.shape, jnp.int32),
            vmem((8, TILE), jnp.int32),
            pltpu.SMEM((8, TILE), jnp.int32),
            vmem((slots_max, TILE, TILE), BF16),
            vmem((slots_max + 1, TILE, TILE), BF16),
            vmem((n_cb, TILE, f), BF16),
            vmem(weight.shape, BF16),
            vmem((Z_HI, ch, hid), BF16),
            vmem((Z_HI, ch, hid), BF16),
            vmem((n_cb * TILE, n_cb * TILE), BF16),
            vmem((slots_max + 1, TILE, f), F32),
            vmem((n_blocks, block_rows, f), F32),
            vmem((n_blocks, n_x, ch, f), BF16),
            vmem((n_blocks, n_x, ch, f), BF16),
            vmem((n_blocks, n_x, ch, f), BF16),
            vmem((Z_HI, ch, f), F32),
            vmem((Z_HI, plane, ch, f), BF16),
            vmem((Z_HI, ch, f), BF16),
            vmem((Z_HI, ch, f), BF16),
            vmem((n_blocks, n_x, CORES, ch, f), BF16),
            vmem((n_cb * TILE, f), F32),
            vmem((n_row, zc, f), BF16),
            vmem((n_row, zc, f), BF16),
            vmem((CORES, plane, piece, TILE), F32),
            vmem((plane, piece, TILE), F32),
            vmem((plane, piece, TILE), F32),
            vmem((n_row, piece, TILE), F32),
            vmem((CORES, plane, piece, TILE), F32),
            dma((2,)),
            dma,
            dma((LOADS + 3,)),
            dma((2,)),
            dma,
            dma((n_blocks,)),
            dma,
            dma((Z_HI, 2)),
            dma,
            dma((Z_HI, 2)),
            dma,
            dma((Z_HI, 2, n_y)),
            dma,
            dma((Z_HI, n_y)),
            dma((2,)),
            dma((2,)),
            dma((2,)),
            dma((2,)),
            dma((2,)),
            dma((2,)),
        ],
        compiler_params=pltpu.CompilerParams(
            collective_id=0, has_side_effects=True, vmem_limit_bytes=40 * 1024 * 1024
        ),
        name="graph_layer",
    )(tile_count, *operands)
    act, ig, weight_grad = pl.pallas_call(
        deliver,
        out_shape=(
            jax.ShapeDtypeStruct((ch, hid), BF16),
            jax.ShapeDtypeStruct((zc, f), BF16),
            jax.ShapeDtypeStruct((f, hid), F32),
        ),
        in_specs=[pl.BlockSpec(memory_space=pltpu.VMEM)] * 3,
        out_specs=(pl.BlockSpec(memory_space=pltpu.HBM),) * 3,
        scratch_shapes=[dma((2 + CORES,))],
        name="deliver",
    )(*[pltpu.with_memory_space_constraint(a, pltpu.VMEM) for a in (act, ig, wg)])
    return act, ig[None], weight_grad


def solution(mesh):
    in_specs = (
        P("row", ("col", "depth"), None, None, None),
        P("row", ("col", "depth"), None),
        P("row", ("col", "depth"), None),
        P("row", ("col", "depth")),
        P(("col", "depth"), None),
        P(),
        P(("row", "col", "depth"), None),
    )
    out_specs = (P(("row", "col", "depth"), None), P(("col", "depth"), "row", None), P())
    return jax.shard_map(local, mesh=mesh, in_specs=in_specs, out_specs=out_specs, check_vma=False)
```

```python
import functools
import math

import jax
import jax.numpy as jnp
from jax import lax
from jax.experimental import pallas as pl
from jax.experimental.pallas import tpu as pltpu
from jax.sharding import PartitionSpec as P

TILE = 128
Z_HI = 2
LOADS = 8
CORES = 2
BF16 = jnp.bfloat16
F32 = jnp.float32


def kernel(
    sizes, count_s, rows_in, cols_in, vals_in, feat_in, w_in, cot_in, act_out, ig_out, wg_out,
    rows_s, cols_s, places, table, vals, valst, feat, w, cot, act, dense, prod, part, sb, rb, qs, own, slots, zsend, zrecv, g, acc,
    xs, xr, wt, wr, wslots, wz, wo,
    slot_sem, table_sem, load_sem, csem, s1s, s1r, s2s, s2r, zs, zr, ga_s, ga_r, gc_s, gc_r,
    xsem, w1, w2, w3, w5, w6,
):
    n_row, n_y, n_x, ch, n_cb, block_tiles, slots_max = sizes
    n_blocks = Z_HI * n_y
    plane = n_x * n_y
    zc = n_cb * TILE // n_row
    row, col, depth = lax.axis_index("row"), lax.axis_index("col"), lax.axis_index("depth")
    zh, y = lax.div(col, n_y), lax.rem(col, n_y)
    x, core = lax.div(depth, CORES), lax.rem(depth, CORES)
    z_other, other = 1 - zh, 1 - core
    here = y * n_x + x

    sibling = (row, col, x * CORES + other)
    partner = (row, z_other * n_y + y, depth)

    def in_plane(dy, dx):
        yy, xx = lax.rem(y + dy, n_y), lax.rem(x + dx, n_x)
        return yy, xx, (row, zh * n_y + yy, xx * CORES + core)

    def in_row(dz):
        rr = lax.rem(row + dz, n_row)
        return rr, (rr, col, depth)

    offsets = [(dy, dx) for dy in range(n_y) for dx in range(n_x) if (dy, dx) != (0, 0)]
    hops = lambda o: (min(o[0], n_y - o[0]), min(o[1], n_x - o[1]))
    offsets.sort(key=lambda o: (-sum(hops(o)), abs(hops(o)[0] - hops(o)[1]), o[0] + o[1]))
    long = (ch // 16 + 1) // 2 * 16
    short = ch - long
    pieces = [
        [pl.ds(0, short), pl.ds(short, long)],
        [pl.ds(0, long), pl.ds(long, short)],
    ]
    units = [(phase, half) for phase in range(Z_HI) for half in range(2)]
    strides = sorted(range(1, n_row), key=lambda dz: -abs(2 * dz - n_row))

    def send(src, dst, send_sem, recv_sem, device):
        pltpu.make_async_remote_copy(
            src_ref=src, dst_ref=dst, send_sem=send_sem, recv_sem=recv_sem,
            device_id=device, device_id_type=pl.DeviceIdType.MESH,
        ).start()

    def wait(ref, sem):
        pltpu.make_async_copy(ref, ref, sem).wait()

    slot_loads = [
        pltpu.make_async_copy(rows_in, rows_s, slot_sem.at[0]),
        pltpu.make_async_copy(cols_in, cols_s, slot_sem.at[1]),
    ]
    part_slots = slots_max // LOADS
    value_loads = []
    for q in range(LOADS):
        span = pl.ds(q * part_slots, part_slots)
        value_loads.append(
            pltpu.make_async_copy(vals_in.at[0, 0, span], vals.at[span], load_sem.at[q])
        )
    feat_load = pltpu.make_async_copy(feat_in, feat, load_sem.at[LOADS])
    late_loads = [
        pltpu.make_async_copy(cot_in, cot.at[zh], load_sem.at[LOADS + 1]),
        pltpu.make_async_copy(w_in, w, load_sem.at[LOADS + 2]),
    ]
    for load in slot_loads + [feat_load] + value_loads + late_loads:
        load.start()

    barrier = pltpu.get_barrier_semaphore()
    peers = [sibling, partner]
    peers += [in_plane(dy, dx)[2] for dy, dx in offsets]
    peers += [in_row(dz)[1] for dz in strides]
    for peer in peers:
        pl.semaphore_signal(barrier, inc=1, device_id=peer, device_id_type=pl.DeviceIdType.MESH)

    valst[slots_max] = jnp.zeros((TILE, TILE), BF16)
    prod[slots_max] = jnp.zeros((TILE, TILE), F32)

    for load in slot_loads:
        load.wait()
    count = count_s[0, 0]
    place = lax.broadcasted_iota(jnp.int32, places.shape, 0) * TILE
    place = place + lax.broadcasted_iota(jnp.int32, places.shape, 1)

    def fill(t, found):
        for u in range(LOADS):
            s = t * LOADS + u
            key = jnp.where(s < count, rows_s[0, 0, s] * n_cb + cols_s[0, 0, s], -1)
            found = jnp.where(place == key, s, found)
        return found

    places[...] = lax.fori_loop(
        0, slots_max // LOADS, fill, jnp.full(places.shape, slots_max, jnp.int32)
    )
    table_copy = pltpu.make_async_copy(places, table, table_sem)
    table_copy.start()

    def slot_at(p):
        return table[lax.div(p, TILE), lax.rem(p, TILE)]

    feat_load.wait()

    for q in range(LOADS):
        value_loads[q].wait()

        def multiply(t, carry):
            for u in range(4):
                s = q * part_slots + 4 * t + u
                prod[s] = jnp.dot(vals[s], feat[cols_s[0, 0, s]], preferred_element_type=F32)
            return carry

        lax.fori_loop(0, part_slots // 4, multiply, 0)
    table_copy.wait()

    def chunk(b, xx, cc):
        return part[b, pl.ds(pl.multiple_of((xx * CORES + cc) * ch, 16), ch), :]

    def gather_products(j, carry):
        b = lax.div(j, n_y) * n_y + lax.rem(y + j, n_y)
        for i in range(block_tiles):
            at = (b * block_tiles + i) * n_cb
            total = prod[slot_at(at)]
            for c in range(1, n_cb):
                total = total + prod[slot_at(at + c)]
            part[b, i * TILE : (i + 1) * TILE, :] = total
        for xx in range(n_x):
            sb[b, xx] = chunk(b, xx, other).astype(BF16)
        send(sb.at[b], rb.at[b], s1s, s1r.at[b], sibling)
        return carry

    pl.semaphore_wait(barrier, len(peers))
    lax.fori_loop(0, n_blocks, gather_products, 0)
    for load in late_loads:
        load.wait()
    send(cot.at[zh], cot.at[zh], csem.at[0], csem.at[1], partner)

    for phase in range(Z_HI):

        def pair(i, carry):
            b = phase * n_y + lax.rem(y + i, n_y)
            wait(rb.at[b], s1r.at[b])
            for xx in range(n_x):
                qs[b, xx] = (chunk(b, xx, core) + rb[b, xx].astype(F32)).astype(BF16)
            return carry

        lax.fori_loop(0, n_y, pair, 0)
        for half, rows in enumerate(pieces[phase]):
            for dy, dx in offsets:
                yy, xx, device = in_plane(dy, dx)
                send(
                    qs.at[phase * n_y + yy, xx, rows], slots.at[phase, dy * n_x + dx, rows],
                    s2s, s2r.at[phase, half], device,
                )
        b = phase * n_y + y
        own[phase] = chunk(b, x, core) + rb[b, x].astype(F32)

    def turn(first, last):
        def step(t, carry):
            for u in range(4):
                valst[4 * t + u] = vals[4 * t + u].T
            return carry

        lax.fori_loop(first // 4, last // 4, step, 0)

    half_slots = slots_max // 8 * 4
    turn(0, half_slots)

    for phase, half in units:
        rows = pieces[phase][half]
        wait(slots.at[phase, pl.ds(1, plane - 1), rows], s2r.at[phase, half])
        total = own[phase, rows]
        for k in range(1, plane):
            total = total + slots[phase, k, rows].astype(F32)
        zsend[phase, rows] = total.astype(BF16)
        mine = zsend.at[phase, rows]
        send(mine, zrecv.at[phase, rows], zs, zr.at[phase, half], partner)
        if (phase, half) == units[0]:
            turn(half_slots, slots_max)

    wait(cot.at[z_other], csem.at[1])

    for phase, half in units:
        rows = pieces[phase][half]
        wait(zrecv.at[phase, rows], zr.at[phase, half])
        agg = (zsend[phase, rows].astype(F32) + zrecv[phase, rows].astype(F32)).astype(BF16)
        pre = jnp.dot(agg, w[...], preferred_element_type=F32)
        sig = jax.nn.sigmoid(pre)
        slope = sig * (1.0 + pre * (1.0 - sig))
        grad_pre = (cot[phase, rows].astype(F32) * slope).astype(BF16)
        grad_agg = lax.dot_general(
            grad_pre, w[...], (((1,), (1,)), ((), ())), preferred_element_type=F32
        )
        mine = g.at[phase * n_y + y, x, core, rows]
        mine[...] = grad_agg.astype(BF16)
        if (phase, half) != units[-1]:
            for dy, dx in offsets:
                send(mine, mine, ga_s, ga_r.at[phase, half, dy], in_plane(dy, dx)[2])
        terms = lax.dot_general(
            agg, grad_pre, (((0,), (0,)), ((), ())), preferred_element_type=F32
        )
        for lane in range(CORES):
            term = terms[:, lane * TILE : (lane + 1) * TILE].reshape(wt.shape[1:])
            wt[lane] = term if (phase, half) == units[0] else wt[lane] + term
        act[phase, rows] = (pre * sig).astype(BF16)

    send(wt.at[other], wr, w1.at[0], w1.at[1], sibling)
    act_out[...] = act[zh]
    wait(wr, w1.at[1])
    wt[core] = wt[core] + wr[...]
    for dy, dx in offsets:
        yy, xx, device = in_plane(dy, dx)
        send(wt.at[core, yy * n_x + xx], wslots.at[dy * n_x + dx], w2.at[0], w2.at[1], device)
    for dy, dx in offsets:
        send(mine, mine, ga_s, ga_r.at[phase, half, dy], in_plane(dy, dx)[2])

    acc[...] = jnp.zeros_like(acc)

    def gather(phase):
        def source(i):
            dy = i + lax.div(i, 2) * (5 - 2 * i)
            return dy, phase * n_y + lax.rem(y + n_y - dy, n_y)

        def step(i, carry):
            @pl.when(i < n_y)
            def _():
                dy, b = source(i)
                group = g.at[b, pl.ds(0, n_x), core]

                for half, rows in enumerate(pieces[phase]):

                    @pl.when(dy == 0)
                    def _():
                        wait(slots.at[0, pl.ds(0, n_x - 1), rows], ga_r.at[phase, half, dy])

                    @pl.when(dy != 0)
                    def _():
                        wait(g.at[b, pl.ds(0, n_x), core, rows], ga_r.at[phase, half, dy])

                send(group, group, gc_s, gc_r.at[phase, dy], sibling)

            @pl.when(i > 0)
            def _():
                dy, b = source(i - 1)
                for c in range(n_cb):
                    for t in range(block_tiles):
                        slot = slot_at((b * block_tiles + t) * n_cb + c)
                        dense[c * TILE : (c + 1) * TILE, t * TILE : (t + 1) * TILE] = valst[slot]
                wait(g.at[b, pl.ds(0, n_x), other], gc_r.at[phase, dy])
                grad = g[b].reshape(block_tiles * TILE, TILE)
                acc[...] += jnp.dot(dense[...], grad, preferred_element_type=F32)

            return carry

        lax.fori_loop(0, n_y + 1, step, 0)

    gather(0)
    wait(wslots.at[pl.ds(1, plane - 1)], w2.at[1])
    piece = wt[core, here]
    for k in range(1, plane):
        piece = piece + wslots[k]
    wz[row] = piece
    for dz in strides:
        send(wz.at[row], wz.at[row], w3.at[0], w3.at[1], in_row(dz)[1])

    gather(1)
    for dz in strides:
        rr, device = in_row(dz)
        xs[rr] = acc[pl.ds(pl.multiple_of(rr * zc, 16), zc), :].astype(BF16)
        send(xs.at[rr], xr.at[dz], xsem.at[0], xsem.at[1], device)

    wait(wz.at[pl.ds(0, n_row - 1)], w3.at[1])
    piece = wz[0]
    for k in range(1, n_row):
        piece = piece + wz[k]
    scale = 1.0 / math.sqrt(n_row * n_blocks * block_tiles * TILE)
    final = wo.at[core, here]
    final[...] = piece * scale
    for dy, dx in offsets:
        send(final, final, w5.at[0], w5.at[1], in_plane(dy, dx)[2])
    wait(wo.at[core, pl.ds(0, plane - 1)], w5.at[1])
    send(wo.at[core], wo.at[core], w6.at[0], w6.at[1], sibling)

    total = acc[pl.ds(pl.multiple_of(row * zc, 16), zc), :]
    wait(xr.at[pl.ds(1, n_row - 1)], xsem.at[1])
    for k in range(1, n_row):
        total = total + xr[k].astype(F32)
    ig_out[...] = total.astype(BF16)
    wait(wo.at[other], w6.at[1])
    for c in range(CORES):
        wg_out[c] = wo[c].reshape(TILE, TILE)

    wait(sb, s1s)
    wait(cot.at[zh], csem.at[0])
    wait(slots.at[:, pl.ds(1, plane - 1)], s2s)
    wait(zsend, zs)
    wait(slots.at[:, pl.ds(1, plane - 1)], ga_s)
    wait(sb, gc_s)
    wait(wt.at[other], w1.at[0])
    wait(wslots.at[pl.ds(1, plane - 1)], w2.at[0])
    wait(wz.at[pl.ds(0, n_row - 1)], w3.at[0])
    wait(wo.at[core, pl.ds(0, plane - 1)], w5.at[0])
    wait(wo.at[core], w6.at[0])
    wait(xr.at[pl.ds(1, n_row - 1)], xsem.at[0])


def deliver(act, ig, wg, act_out, ig_out, wg_out, sem):
    copies = [
        pltpu.make_async_copy(act, act_out, sem.at[0]),
        pltpu.make_async_copy(ig, ig_out, sem.at[1]),
    ]
    for c in range(CORES):
        lanes = pl.ds(c * TILE, TILE)
        copies.append(pltpu.make_async_copy(wg.at[c], wg_out.at[:, lanes], sem.at[2 + c]))
    for copy in copies:
        copy.start()
    for copy in copies:
        copy.wait()


def local(tile_values, tile_rows, tile_cols, tile_count, features, weight, cotangent):
    n_row, n_col, n_depth = lax.axis_size("row"), lax.axis_size("col"), lax.axis_size("depth")
    n_y, n_x = n_col // Z_HI, n_depth // CORES
    ch, hid = cotangent.shape
    f = features.shape[1]
    n_cb = features.shape[0] // TILE
    n_blocks = n_col
    block_rows = n_depth * ch
    block_tiles = block_rows // TILE
    slots_max = tile_values.shape[2]
    plane = n_x * n_y
    zc = features.shape[0] // n_row
    piece = f // plane

    sizes = (n_row, n_y, n_x, ch, n_cb, block_tiles, slots_max)
    vmem, dma = pltpu.VMEM, pltpu.SemaphoreType.DMA
    operands = [
        pltpu.with_memory_space_constraint(a, pltpu.HBM)
        for a in (
            tile_rows, tile_cols, tile_values, features.reshape(n_cb, TILE, f),
            weight, cotangent,
        )
    ]
    anywhere = pl.BlockSpec(memory_space=pl.ANY)
    act, ig, wg = pl.pallas_call(
        functools.partial(kernel, sizes),
        out_shape=(
            vmem((ch, hid), BF16),
            vmem((zc, f), BF16),
            vmem((CORES, f, TILE), F32),
        ),
        in_specs=[pl.BlockSpec(memory_space=pltpu.SMEM)]
        + [pl.BlockSpec(memory_space=pltpu.HBM)] * 6,
        out_specs=(pl.BlockSpec(memory_space=pltpu.VMEM),) * 3,
        scratch_shapes=[
            pltpu.SMEM(tile_rows.shape, jnp.int32),
            pltpu.SMEM(tile_cols.shape, jnp.int32),
            vmem((8, TILE), jnp.int32),
            pltpu.SMEM((8, TILE), jnp.int32),
            vmem((slots_max, TILE, TILE), BF16),
            vmem((slots_max + 1, TILE, TILE), BF16),
            vmem((n_cb, TILE, f), BF16),
            vmem(weight.shape, BF16),
            vmem((Z_HI, ch, hid), BF16),
            vmem((Z_HI, ch, hid), BF16),
            vmem((n_cb * TILE, n_cb * TILE), BF16),
            vmem((slots_max + 1, TILE, f), F32),
            vmem((n_blocks, block_rows, f), F32),
            vmem((n_blocks, n_x, ch, f), BF16),
            vmem((n_blocks, n_x, ch, f), BF16),
            vmem((n_blocks, n_x, ch, f), BF16),
            vmem((Z_HI, ch, f), F32),
            vmem((Z_HI, plane, ch, f), BF16),
            vmem((Z_HI, ch, f), BF16),
            vmem((Z_HI, ch, f), BF16),
            vmem((n_blocks, n_x, CORES, ch, f), BF16),
            vmem((n_cb * TILE, f), F32),
            vmem((n_row, zc, f), BF16),
            vmem((n_row, zc, f), BF16),
            vmem((CORES, plane, piece, TILE), F32),
            vmem((plane, piece, TILE), F32),
            vmem((plane, piece, TILE), F32),
            vmem((n_row, piece, TILE), F32),
            vmem((CORES, plane, piece, TILE), F32),
            dma((2,)),
            dma,
            dma((LOADS + 3,)),
            dma((2,)),
            dma,
            dma((n_blocks,)),
            dma,
            dma((Z_HI, 2)),
            dma,
            dma((Z_HI, 2)),
            dma,
            dma((Z_HI, 2, n_y)),
            dma,
            dma((Z_HI, n_y)),
            dma((2,)),
            dma((2,)),
            dma((2,)),
            dma((2,)),
            dma((2,)),
            dma((2,)),
        ],
        compiler_params=pltpu.CompilerParams(
            collective_id=0, has_side_effects=True, vmem_limit_bytes=40 * 1024 * 1024
        ),
        name="graph_layer",
    )(tile_count, *operands)
    act, ig, weight_grad = pl.pallas_call(
        deliver,
        out_shape=(
            jax.ShapeDtypeStruct((ch, hid), BF16),
            jax.ShapeDtypeStruct((zc, f), BF16),
            jax.ShapeDtypeStruct((f, hid), F32),
        ),
        in_specs=[pl.BlockSpec(memory_space=pltpu.VMEM)] * 3,
        out_specs=(pl.BlockSpec(memory_space=pltpu.HBM),) * 3,
        scratch_shapes=[dma((2 + CORES,))],
        name="deliver",
    )(*[pltpu.with_memory_space_constraint(a, pltpu.VMEM) for a in (act, ig, wg)])
    return act, ig[None], weight_grad


def solution(mesh):
    in_specs = (
        P("row", ("col", "depth"), None, None, None),
        P("row", ("col", "depth"), None),
        P("row", ("col", "depth"), None),
        P("row", ("col", "depth")),
        P(("col", "depth"), None),
        P(),
        P(("row", "col", "depth"), None),
    )
    out_specs = (P(("row", "col", "depth"), None), P(("col", "depth"), "row", None), P())
    return jax.shard_map(local, mesh=mesh, in_specs=in_specs, out_specs=out_specs, check_vma=False)
```

```python
import functools
import math

import jax
import jax.numpy as jnp
from jax import lax
from jax.experimental import pallas as pl
from jax.experimental.pallas import tpu as pltpu
from jax.sharding import PartitionSpec as P

TILE = 128
Z_HI = 2
LOADS = 8
CORES = 2
BF16 = jnp.bfloat16
F32 = jnp.float32


def kernel(
    sizes, count_s, rows_in, cols_in, vals_in, feat_in, w_in, cot_in, act_out, ig_out, wg_out,
    rows_s, cols_s, places, table, vals, valst, feat, w, cot, act, dense, prod, part, sb, rb, qs, own, slots, zsend, zrecv, g, acc,
    xs, xr, wt, wr, wslots, wz, wo,
    slot_sem, table_sem, load_sem, csem, s1s, s1r, s2s, s2r, zs, zr, ga_s, ga_r, gc_s, gc_r,
    xsem, w1, w2, w3, w5, w6,
):
    n_row, n_y, n_x, ch, n_cb, block_tiles, slots_max = sizes
    n_blocks = Z_HI * n_y
    plane = n_x * n_y
    zc = n_cb * TILE // n_row
    row, col, depth = lax.axis_index("row"), lax.axis_index("col"), lax.axis_index("depth")
    zh, y = lax.div(col, n_y), lax.rem(col, n_y)
    x, core = lax.div(depth, CORES), lax.rem(depth, CORES)
    z_other, other = 1 - zh, 1 - core
    here = y * n_x + x

    sibling = (row, col, x * CORES + other)
    partner = (row, z_other * n_y + y, depth)

    def in_plane(dy, dx):
        yy, xx = lax.rem(y + dy, n_y), lax.rem(x + dx, n_x)
        return yy, xx, (row, zh * n_y + yy, xx * CORES + core)

    def in_row(dz):
        rr = lax.rem(row + dz, n_row)
        return rr, (rr, col, depth)

    offsets = [(dy, dx) for dy in range(n_y) for dx in range(n_x) if (dy, dx) != (0, 0)]
    hops = lambda o: (min(o[0], n_y - o[0]), min(o[1], n_x - o[1]))
    offsets.sort(key=lambda o: (-sum(hops(o)), abs(hops(o)[0] - hops(o)[1]), o[0] + o[1]))
    long = (ch // 16 + 1) // 2 * 16
    short = ch - long
    pieces = [
        [pl.ds(0, short), pl.ds(short, long)],
        [pl.ds(0, long), pl.ds(long, short)],
    ]
    units = [(phase, half) for phase in range(Z_HI) for half in range(2)]
    strides = sorted(range(1, n_row), key=lambda dz: -abs(2 * dz - n_row))

    def send(src, dst, send_sem, recv_sem, device):
        pltpu.make_async_remote_copy(
            src_ref=src, dst_ref=dst, send_sem=send_sem, recv_sem=recv_sem,
            device_id=device, device_id_type=pl.DeviceIdType.MESH,
        ).start()

    def wait(ref, sem):
        pltpu.make_async_copy(ref, ref, sem).wait()

    slot_loads = [
        pltpu.make_async_copy(rows_in, rows_s, slot_sem.at[0]),
        pltpu.make_async_copy(cols_in, cols_s, slot_sem.at[1]),
    ]
    part_slots = slots_max // LOADS
    value_loads = []
    for q in range(LOADS):
        span = pl.ds(q * part_slots, part_slots)
        value_loads.append(
            pltpu.make_async_copy(vals_in.at[0, 0, span], vals.at[span], load_sem.at[q])
        )
    feat_load = pltpu.make_async_copy(feat_in, feat, load_sem.at[LOADS])
    late_loads = [
        pltpu.make_async_copy(cot_in, cot.at[zh], load_sem.at[LOADS + 1]),
        pltpu.make_async_copy(w_in, w, load_sem.at[LOADS + 2]),
    ]
    for load in slot_loads + [feat_load] + value_loads + late_loads:
        load.start()

    barrier = pltpu.get_barrier_semaphore()
    peers = [sibling, partner]
    peers += [in_plane(dy, dx)[2] for dy, dx in offsets]
    peers += [in_row(dz)[1] for dz in strides]
    for peer in peers:
        pl.semaphore_signal(barrier, inc=1, device_id=peer, device_id_type=pl.DeviceIdType.MESH)

    valst[slots_max] = jnp.zeros((TILE, TILE), BF16)
    prod[slots_max] = jnp.zeros((TILE, TILE), F32)

    for load in slot_loads:
        load.wait()
    count = count_s[0, 0]
    place = lax.broadcasted_iota(jnp.int32, places.shape, 0) * TILE
    place = place + lax.broadcasted_iota(jnp.int32, places.shape, 1)

    def fill(t, found):
        for u in range(LOADS):
            s = t * LOADS + u
            key = jnp.where(s < count, rows_s[0, 0, s] * n_cb + cols_s[0, 0, s], -1)
            found = jnp.where(place == key, s, found)
        return found

    places[...] = lax.fori_loop(
        0, slots_max // LOADS, fill, jnp.full(places.shape, slots_max, jnp.int32)
    )
    table_copy = pltpu.make_async_copy(places, table, table_sem)
    table_copy.start()

    def slot_at(p):
        return table[lax.div(p, TILE), lax.rem(p, TILE)]

    feat_load.wait()

    for q in range(LOADS):
        value_loads[q].wait()

        def multiply(t, carry):
            for u in range(4):
                s = q * part_slots + 4 * t + u
                prod[s] = jnp.dot(vals[s], feat[cols_s[0, 0, s]], preferred_element_type=F32)
            return carry

        lax.fori_loop(0, part_slots // 4, multiply, 0)
    table_copy.wait()

    def chunk(b, xx, cc):
        return part[b, pl.ds(pl.multiple_of((xx * CORES + cc) * ch, 16), ch), :]

    def gather_products(j, carry):
        b = lax.div(j, n_y) * n_y + lax.rem(y + j, n_y)
        for i in range(block_tiles):
            at = (b * block_tiles + i) * n_cb
            total = prod[slot_at(at)]
            for c in range(1, n_cb):
                total = total + prod[slot_at(at + c)]
            part[b, i * TILE : (i + 1) * TILE, :] = total
        for xx in range(n_x):
            sb[b, xx] = chunk(b, xx, other).astype(BF16)
        send(sb.at[b], rb.at[b], s1s, s1r.at[b], sibling)
        return carry

    pl.semaphore_wait(barrier, len(peers))
    lax.fori_loop(0, n_blocks, gather_products, 0)
    for load in late_loads:
        load.wait()
    send(cot.at[zh], cot.at[zh], csem.at[0], csem.at[1], partner)

    for phase in range(Z_HI):

        def pair(i, carry):
            b = phase * n_y + lax.rem(y + i, n_y)
            wait(rb.at[b], s1r.at[b])
            for xx in range(n_x):
                qs[b, xx] = (chunk(b, xx, core) + rb[b, xx].astype(F32)).astype(BF16)
            return carry

        lax.fori_loop(0, n_y, pair, 0)
        for half, rows in enumerate(pieces[phase]):
            for dy, dx in offsets:
                yy, xx, device = in_plane(dy, dx)
                send(
                    qs.at[phase * n_y + yy, xx, rows], slots.at[phase, dy * n_x + dx, rows],
                    s2s, s2r.at[phase, half], device,
                )
        b = phase * n_y + y
        own[phase] = chunk(b, x, core) + rb[b, x].astype(F32)

    def turn(first, last):
        def step(t, carry):
            for u in range(4):
                valst[4 * t + u] = vals[4 * t + u].T
            return carry

        lax.fori_loop(first // 4, last // 4, step, 0)

    turn(0, slots_max)

    def spread_tiles(first, last):
        def step(b, carry):
            for c in range(n_cb):
                for t in range(block_tiles):
                    slot = slot_at((b * block_tiles + t) * n_cb + c)
                    dense[b, c * TILE : (c + 1) * TILE, t * TILE : (t + 1) * TILE] = valst[slot]
            return carry

        lax.fori_loop(first, last, step, 0)

    for phase, half in units:
        rows = pieces[phase][half]
        wait(slots.at[phase, pl.ds(1, plane - 1), rows], s2r.at[phase, half])
        total = own[phase, rows]
        for k in range(1, plane):
            total = total + slots[phase, k, rows].astype(F32)
        zsend[phase, rows] = total.astype(BF16)
        mine = zsend.at[phase, rows]
        send(mine, zrecv.at[phase, rows], zs, zr.at[phase, half], partner)
        done = units.index((phase, half))
        spread_tiles(n_blocks * done // len(units), n_blocks * (done + 1) // len(units))

    wait(cot.at[z_other], csem.at[1])

    for phase, half in units:
        rows = pieces[phase][half]
        wait(zrecv.at[phase, rows], zr.at[phase, half])
        agg = (zsend[phase, rows].astype(F32) + zrecv[phase, rows].astype(F32)).astype(BF16)
        pre = jnp.dot(agg, w[...], preferred_element_type=F32)
        sig = jax.nn.sigmoid(pre)
        slope = sig * (1.0 + pre * (1.0 - sig))
        grad_pre = (cot[phase, rows].astype(F32) * slope).astype(BF16)
        grad_agg = lax.dot_general(
            grad_pre, w[...], (((1,), (1,)), ((), ())), preferred_element_type=F32
        )
        mine = g.at[phase * n_y + y, x, core, rows]
        mine[...] = grad_agg.astype(BF16)
        if (phase, half) != units[-1]:
            for dy, dx in offsets:
                send(mine, mine, ga_s, ga_r.at[phase, half, dy], in_plane(dy, dx)[2])
        terms = lax.dot_general(
            agg, grad_pre, (((0,), (0,)), ((), ())), preferred_element_type=F32
        )
        for lane in range(CORES):
            term = terms[:, lane * TILE : (lane + 1) * TILE].reshape(wt.shape[1:])
            wt[lane] = term if (phase, half) == units[0] else wt[lane] + term
        act[phase, rows] = (pre * sig).astype(BF16)

    send(wt.at[other], wr, w1.at[0], w1.at[1], sibling)
    act_out[...] = act[zh]
    wait(wr, w1.at[1])
    wt[core] = wt[core] + wr[...]
    for dy, dx in offsets:
        yy, xx, device = in_plane(dy, dx)
        send(wt.at[core, yy * n_x + xx], wslots.at[dy * n_x + dx], w2.at[0], w2.at[1], device)
    for dy, dx in offsets:
        send(mine, mine, ga_s, ga_r.at[phase, half, dy], in_plane(dy, dx)[2])

    acc[...] = jnp.zeros_like(acc)

    def gather(phase):
        def source(i):
            dy = i + lax.div(i, 2) * (5 - 2 * i)
            return dy, phase * n_y + lax.rem(y + n_y - dy, n_y)

        def pass_on(i, carry):
            dy, b = source(i)
            group = g.at[b, pl.ds(0, n_x), core]
            for half, rows in enumerate(pieces[phase]):

                @pl.when(dy == 0)
                def _():
                    wait(slots.at[0, pl.ds(0, n_x - 1), rows], ga_r.at[phase, half, dy])

                @pl.when(dy != 0)
                def _():
                    wait(g.at[b, pl.ds(0, n_x), core, rows], ga_r.at[phase, half, dy])

            send(group, group, gc_s, gc_r.at[phase, dy], sibling)
            return carry

        def multiply(i, carry):
            dy, b = source(i)
            wait(g.at[b, pl.ds(0, n_x), other], gc_r.at[phase, dy])
            grad = g[b].reshape(block_tiles * TILE, TILE)
            for c in range(n_cb):
                at = pl.ds(c * TILE, TILE)
                acc[at, :] += jnp.dot(dense[b, at, :], grad, preferred_element_type=F32)
            return carry

        lax.fori_loop(0, n_y, pass_on, 0)
        lax.fori_loop(0, n_y, multiply, 0)

    gather(0)
    wait(wslots.at[pl.ds(1, plane - 1)], w2.at[1])
    piece = wt[core, here]
    for k in range(1, plane):
        piece = piece + wslots[k]
    wz[row] = piece
    for dz in strides:
        send(wz.at[row], wz.at[row], w3.at[0], w3.at[1], in_row(dz)[1])

    gather(1)
    for dz in strides:
        rr, device = in_row(dz)
        xs[rr] = acc[pl.ds(pl.multiple_of(rr * zc, 16), zc), :].astype(BF16)
        send(xs.at[rr], xr.at[dz], xsem.at[0], xsem.at[1], device)

    wait(wz.at[pl.ds(0, n_row - 1)], w3.at[1])
    piece = wz[0]
    for k in range(1, n_row):
        piece = piece + wz[k]
    scale = 1.0 / math.sqrt(n_row * n_blocks * block_tiles * TILE)
    final = wo.at[core, here]
    final[...] = piece * scale
    for dy, dx in offsets:
        send(final, final, w5.at[0], w5.at[1], in_plane(dy, dx)[2])
    wait(wo.at[core, pl.ds(0, plane - 1)], w5.at[1])
    send(wo.at[core], wo.at[core], w6.at[0], w6.at[1], sibling)

    total = acc[pl.ds(pl.multiple_of(row * zc, 16), zc), :]
    wait(xr.at[pl.ds(1, n_row - 1)], xsem.at[1])
    for k in range(1, n_row):
        total = total + xr[k].astype(F32)
    ig_out[...] = total.astype(BF16)
    wait(wo.at[other], w6.at[1])
    for c in range(CORES):
        wg_out[c] = wo[c].reshape(TILE, TILE)

    wait(sb, s1s)
    wait(cot.at[zh], csem.at[0])
    wait(slots.at[:, pl.ds(1, plane - 1)], s2s)
    wait(zsend, zs)
    wait(slots.at[:, pl.ds(1, plane - 1)], ga_s)
    wait(sb, gc_s)
    wait(wt.at[other], w1.at[0])
    wait(wslots.at[pl.ds(1, plane - 1)], w2.at[0])
    wait(wz.at[pl.ds(0, n_row - 1)], w3.at[0])
    wait(wo.at[core, pl.ds(0, plane - 1)], w5.at[0])
    wait(wo.at[core], w6.at[0])
    wait(xr.at[pl.ds(1, n_row - 1)], xsem.at[0])


def deliver(act, ig, wg, act_out, ig_out, wg_out, sem):
    copies = [
        pltpu.make_async_copy(act, act_out, sem.at[0]),
        pltpu.make_async_copy(ig, ig_out, sem.at[1]),
    ]
    for c in range(CORES):
        lanes = pl.ds(c * TILE, TILE)
        copies.append(pltpu.make_async_copy(wg.at[c], wg_out.at[:, lanes], sem.at[2 + c]))
    for copy in copies:
        copy.start()
    for copy in copies:
        copy.wait()


def local(tile_values, tile_rows, tile_cols, tile_count, features, weight, cotangent):
    n_row, n_col, n_depth = lax.axis_size("row"), lax.axis_size("col"), lax.axis_size("depth")
    n_y, n_x = n_col // Z_HI, n_depth // CORES
    ch, hid = cotangent.shape
    f = features.shape[1]
    n_cb = features.shape[0] // TILE
    n_blocks = n_col
    block_rows = n_depth * ch
    block_tiles = block_rows // TILE
    slots_max = tile_values.shape[2]
    plane = n_x * n_y
    zc = features.shape[0] // n_row
    piece = f // plane

    sizes = (n_row, n_y, n_x, ch, n_cb, block_tiles, slots_max)
    vmem, dma = pltpu.VMEM, pltpu.SemaphoreType.DMA
    operands = [
        pltpu.with_memory_space_constraint(a, pltpu.HBM)
        for a in (
            tile_rows, tile_cols, tile_values, features.reshape(n_cb, TILE, f),
            weight, cotangent,
        )
    ]
    anywhere = pl.BlockSpec(memory_space=pl.ANY)
    act, ig, wg = pl.pallas_call(
        functools.partial(kernel, sizes),
        out_shape=(
            vmem((ch, hid), BF16),
            vmem((zc, f), BF16),
            vmem((CORES, f, TILE), F32),
        ),
        in_specs=[pl.BlockSpec(memory_space=pltpu.SMEM)]
        + [pl.BlockSpec(memory_space=pltpu.HBM)] * 6,
        out_specs=(pl.BlockSpec(memory_space=pltpu.VMEM),) * 3,
        scratch_shapes=[
            pltpu.SMEM(tile_rows.shape, jnp.int32),
            pltpu.SMEM(tile_cols.shape, jnp.int32),
            vmem((8, TILE), jnp.int32),
            pltpu.SMEM((8, TILE), jnp.int32),
            vmem((slots_max, TILE, TILE), BF16),
            vmem((slots_max + 1, TILE, TILE), BF16),
            vmem((n_cb, TILE, f), BF16),
            vmem(weight.shape, BF16),
            vmem((Z_HI, ch, hid), BF16),
            vmem((Z_HI, ch, hid), BF16),
            vmem((n_blocks, n_cb * TILE, block_rows), BF16),
            vmem((slots_max + 1, TILE, f), F32),
            vmem((n_blocks, block_rows, f), F32),
            vmem((n_blocks, n_x, ch, f), BF16),
            vmem((n_blocks, n_x, ch, f), BF16),
            vmem((n_blocks, n_x, ch, f), BF16),
            vmem((Z_HI, ch, f), F32),
            vmem((Z_HI, plane, ch, f), BF16),
            vmem((Z_HI, ch, f), BF16),
            vmem((Z_HI, ch, f), BF16),
            vmem((n_blocks, n_x, CORES, ch, f), BF16),
            vmem((n_cb * TILE, f), F32),
            vmem((n_row, zc, f), BF16),
            vmem((n_row, zc, f), BF16),
            vmem((CORES, plane, piece, TILE), F32),
            vmem((plane, piece, TILE), F32),
            vmem((plane, piece, TILE), F32),
            vmem((n_row, piece, TILE), F32),
            vmem((CORES, plane, piece, TILE), F32),
            dma((2,)),
            dma,
            dma((LOADS + 3,)),
            dma((2,)),
            dma,
            dma((n_blocks,)),
            dma,
            dma((Z_HI, 2)),
            dma,
            dma((Z_HI, 2)),
            dma,
            dma((Z_HI, 2, n_y)),
            dma,
            dma((Z_HI, n_y)),
            dma((2,)),
            dma((2,)),
            dma((2,)),
            dma((2,)),
            dma((2,)),
            dma((2,)),
        ],
        compiler_params=pltpu.CompilerParams(
            collective_id=0, has_side_effects=True, vmem_limit_bytes=40 * 1024 * 1024
        ),
        name="graph_layer",
    )(tile_count, *operands)
    act, ig, weight_grad = pl.pallas_call(
        deliver,
        out_shape=(
            jax.ShapeDtypeStruct((ch, hid), BF16),
            jax.ShapeDtypeStruct((zc, f), BF16),
            jax.ShapeDtypeStruct((f, hid), F32),
        ),
        in_specs=[pl.BlockSpec(memory_space=pltpu.VMEM)] * 3,
        out_specs=(pl.BlockSpec(memory_space=pltpu.HBM),) * 3,
        scratch_shapes=[dma((2 + CORES,))],
        name="deliver",
    )(*[pltpu.with_memory_space_constraint(a, pltpu.VMEM) for a in (act, ig, wg)])
    return act, ig[None], weight_grad


def solution(mesh):
    in_specs = (
        P("row", ("col", "depth"), None, None, None),
        P("row", ("col", "depth"), None),
        P("row", ("col", "depth"), None),
        P("row", ("col", "depth")),
        P(("col", "depth"), None),
        P(),
        P(("row", "col", "depth"), None),
    )
    out_specs = (P(("row", "col", "depth"), None), P(("col", "depth"), "row", None), P())
    return jax.shard_map(local, mesh=mesh, in_specs=in_specs, out_specs=out_specs, check_vma=False)
```

```python
import functools
import math

import jax
import jax.numpy as jnp
from jax import lax
from jax.experimental import pallas as pl
from jax.experimental.pallas import tpu as pltpu
from jax.sharding import PartitionSpec as P

TILE = 128
Z_HI = 2
LOADS = 8
CORES = 2
BF16 = jnp.bfloat16
F32 = jnp.float32


def kernel(
    sizes, count_s, rows_in, cols_in, vals_in, feat_in, w_in, cot_in, act_out, ig_out, wg_out,
    rows_s, cols_s, places, table, vals, valst, feat, w, cot, act, dense, prod, part, sb, rb, qs, own, slots, zsend, zrecv, g, acc,
    xs, xr, wt, wr, wslots, wz, wo,
    slot_sem, table_sem, load_sem, csem, s1s, s1r, s2s, s2r, zs, zr, ga_s, ga_r, gc_s, gc_r,
    xsem, w1, w2, w3, w5, w6,
):
    n_row, n_y, n_x, ch, n_cb, block_tiles, slots_max = sizes
    n_blocks = Z_HI * n_y
    plane = n_x * n_y
    zc = n_cb * TILE // n_row
    row, col, depth = lax.axis_index("row"), lax.axis_index("col"), lax.axis_index("depth")
    zh, y = lax.div(col, n_y), lax.rem(col, n_y)
    x, core = lax.div(depth, CORES), lax.rem(depth, CORES)
    z_other, other = 1 - zh, 1 - core
    here = y * n_x + x

    sibling = (row, col, x * CORES + other)
    partner = (row, z_other * n_y + y, depth)

    def in_plane(dy, dx):
        yy, xx = lax.rem(y + dy, n_y), lax.rem(x + dx, n_x)
        return yy, xx, (row, zh * n_y + yy, xx * CORES + core)

    def in_row(dz):
        rr = lax.rem(row + dz, n_row)
        return rr, (rr, col, depth)

    offsets = [(dy, dx) for dy in range(n_y) for dx in range(n_x) if (dy, dx) != (0, 0)]
    hops = lambda o: (min(o[0], n_y - o[0]), min(o[1], n_x - o[1]))
    offsets.sort(key=lambda o: (-sum(hops(o)), abs(hops(o)[0] - hops(o)[1]), o[0] + o[1]))
    long = (ch // 16 + 1) // 2 * 16
    short = ch - long
    pieces = [
        [pl.ds(0, short), pl.ds(short, long)],
        [pl.ds(0, long), pl.ds(long, short)],
    ]
    units = [(phase, half) for phase in range(Z_HI) for half in range(2)]
    strides = sorted(range(1, n_row), key=lambda dz: -abs(2 * dz - n_row))

    def send(src, dst, send_sem, recv_sem, device):
        pltpu.make_async_remote_copy(
            src_ref=src, dst_ref=dst, send_sem=send_sem, recv_sem=recv_sem,
            device_id=device, device_id_type=pl.DeviceIdType.MESH,
        ).start()

    def wait(ref, sem):
        pltpu.make_async_copy(ref, ref, sem).wait()

    slot_loads = [
        pltpu.make_async_copy(rows_in, rows_s, slot_sem.at[0]),
        pltpu.make_async_copy(cols_in, cols_s, slot_sem.at[1]),
    ]
    part_slots = slots_max // LOADS
    value_loads = []
    for q in range(LOADS):
        span = pl.ds(q * part_slots, part_slots)
        value_loads.append(
            pltpu.make_async_copy(vals_in.at[0, 0, span], vals.at[span], load_sem.at[q])
        )
    feat_load = pltpu.make_async_copy(feat_in, feat, load_sem.at[LOADS])
    late_loads = [
        pltpu.make_async_copy(cot_in, cot.at[zh], load_sem.at[LOADS + 1]),
        pltpu.make_async_copy(w_in, w, load_sem.at[LOADS + 2]),
    ]
    for load in slot_loads + [feat_load] + value_loads + late_loads:
        load.start()

    barrier = pltpu.get_barrier_semaphore()
    peers = [sibling, partner]
    peers += [in_plane(dy, dx)[2] for dy, dx in offsets]
    peers += [in_row(dz)[1] for dz in strides]
    for peer in peers:
        pl.semaphore_signal(barrier, inc=1, device_id=peer, device_id_type=pl.DeviceIdType.MESH)

    valst[slots_max] = jnp.zeros((TILE, TILE), BF16)
    prod[slots_max] = jnp.zeros((TILE, TILE), F32)

    for load in slot_loads:
        load.wait()
    count = count_s[0, 0]
    place = lax.broadcasted_iota(jnp.int32, places.shape, 0) * TILE
    place = place + lax.broadcasted_iota(jnp.int32, places.shape, 1)

    def fill(t, found):
        for u in range(LOADS):
            s = t * LOADS + u
            key = jnp.where(s < count, rows_s[0, 0, s] * n_cb + cols_s[0, 0, s], -1)
            found = jnp.where(place == key, s, found)
        return found

    places[...] = lax.fori_loop(
        0, slots_max // LOADS, fill, jnp.full(places.shape, slots_max, jnp.int32)
    )
    table_copy = pltpu.make_async_copy(places, table, table_sem)
    table_copy.start()

    def slot_at(p):
        return table[lax.div(p, TILE), lax.rem(p, TILE)]

    feat_load.wait()

    for q in range(LOADS):
        value_loads[q].wait()

        def multiply(t, carry):
            for u in range(4):
                s = q * part_slots + 4 * t + u
                prod[s] = jnp.dot(vals[s], feat[cols_s[0, 0, s]], preferred_element_type=F32)
            return carry

        lax.fori_loop(0, part_slots // 4, multiply, 0)
    table_copy.wait()

    def chunk(b, xx, cc):
        return part[b, pl.ds(pl.multiple_of((xx * CORES + cc) * ch, 16), ch), :]

    def block_of(j):
        return lax.div(j, n_y) * n_y + lax.rem(y + j + n_y // 2, n_y)

    def gather_products(j, carry):
        b = block_of(j)
        for i in range(block_tiles):
            at = (b * block_tiles + i) * n_cb
            total = prod[slot_at(at)]
            for c in range(1, n_cb):
                total = total + prod[slot_at(at + c)]
            part[b, i * TILE : (i + 1) * TILE, :] = total
        for xx in range(n_x):
            sb[b, xx] = chunk(b, xx, other).astype(BF16)
        return carry

    def to_sibling(j, carry):
        b = block_of(j)
        send(sb.at[b], rb.at[b], s1s, s1r.at[b], sibling)
        return carry

    lax.fori_loop(0, n_y, gather_products, 0)
    pl.semaphore_wait(barrier, len(peers))
    lax.fori_loop(0, n_y, to_sibling, 0)
    lax.fori_loop(
        n_y, n_blocks, lambda j, carry: to_sibling(j, gather_products(j, carry)), 0
    )
    for load in late_loads:
        load.wait()
    send(cot.at[zh], cot.at[zh], csem.at[0], csem.at[1], partner)

    for phase in range(Z_HI):

        def pair(i, carry):
            b = block_of(phase * n_y + i)
            wait(rb.at[b], s1r.at[b])
            for xx in range(n_x):
                qs[b, xx] = (chunk(b, xx, core) + rb[b, xx].astype(F32)).astype(BF16)
            dy = lax.rem(i + n_y // 2, n_y)
            rows = pieces[phase][0]
            for dx in range(n_x):
                _, xx, device = in_plane(dy, dx)

                @pl.when(dy + dx > 0)
                def _():
                    send(
                        qs.at[b, xx, rows], slots.at[phase, dy * n_x + dx, rows],
                        s2s, s2r.at[phase, 0], device,
                    )

            return carry

        lax.fori_loop(0, n_y, pair, 0)
        for half, rows in list(enumerate(pieces[phase]))[1:]:
            for dy, dx in offsets:
                yy, xx, device = in_plane(dy, dx)
                send(
                    qs.at[phase * n_y + yy, xx, rows], slots.at[phase, dy * n_x + dx, rows],
                    s2s, s2r.at[phase, half], device,
                )
        b = phase * n_y + y
        own[phase] = chunk(b, x, core) + rb[b, x].astype(F32)

    def turn(first, last):
        def step(t, carry):
            for u in range(4):
                valst[4 * t + u] = vals[4 * t + u].T
            return carry

        lax.fori_loop(first // 4, last // 4, step, 0)

    turn(0, slots_max)

    def spread_tiles(first, last):
        def step(b, carry):
            for c in range(n_cb):
                for t in range(block_tiles):
                    slot = slot_at((b * block_tiles + t) * n_cb + c)
                    dense[b, c * TILE : (c + 1) * TILE, t * TILE : (t + 1) * TILE] = valst[slot]
            return carry

        lax.fori_loop(first, last, step, 0)

    for phase, half in units:
        rows = pieces[phase][half]
        wait(slots.at[phase, pl.ds(1, plane - 1), rows], s2r.at[phase, half])
        total = own[phase, rows]
        for k in range(1, plane):
            total = total + slots[phase, k, rows].astype(F32)
        zsend[phase, rows] = total.astype(BF16)
        mine = zsend.at[phase, rows]
        send(mine, zrecv.at[phase, rows], zs, zr.at[phase, half], partner)
        done = units.index((phase, half))
        spread_tiles(n_blocks * done // len(units), n_blocks * (done + 1) // len(units))

    wait(cot.at[z_other], csem.at[1])

    for phase, half in units:
        rows = pieces[phase][half]
        wait(zrecv.at[phase, rows], zr.at[phase, half])
        agg = (zsend[phase, rows].astype(F32) + zrecv[phase, rows].astype(F32)).astype(BF16)
        pre = jnp.dot(agg, w[...], preferred_element_type=F32)
        sig = jax.nn.sigmoid(pre)
        slope = sig * (1.0 + pre * (1.0 - sig))
        grad_pre = (cot[phase, rows].astype(F32) * slope).astype(BF16)
        grad_agg = lax.dot_general(
            grad_pre, w[...], (((1,), (1,)), ((), ())), preferred_element_type=F32
        )
        mine = g.at[phase * n_y + y, x, core, rows]
        mine[...] = grad_agg.astype(BF16)
        if (phase, half) != units[-1]:
            for dy, dx in offsets:
                send(mine, mine, ga_s, ga_r.at[phase, half, dy], in_plane(dy, dx)[2])
        terms = lax.dot_general(
            agg, grad_pre, (((0,), (0,)), ((), ())), preferred_element_type=F32
        )
        for lane in range(CORES):
            term = terms[:, lane * TILE : (lane + 1) * TILE].reshape(wt.shape[1:])
            wt[lane] = term if (phase, half) == units[0] else wt[lane] + term
        act[phase, rows] = (pre * sig).astype(BF16)

    send(wt.at[other], wr, w1.at[0], w1.at[1], sibling)
    act_out[...] = act[zh]
    wait(wr, w1.at[1])
    wt[core] = wt[core] + wr[...]
    for dy, dx in offsets:
        yy, xx, device = in_plane(dy, dx)
        send(wt.at[core, yy * n_x + xx], wslots.at[dy * n_x + dx], w2.at[0], w2.at[1], device)
    for dy, dx in offsets:
        send(mine, mine, ga_s, ga_r.at[phase, half, dy], in_plane(dy, dx)[2])

    acc[...] = jnp.zeros_like(acc)

    def gather(phase):
        def source(i):
            dy = i + lax.div(i, 2) * (5 - 2 * i)
            return dy, phase * n_y + lax.rem(y + n_y - dy, n_y)

        def pass_on(i, carry):
            dy, b = source(i)
            group = g.at[b, pl.ds(0, n_x), core]
            for half, rows in enumerate(pieces[phase]):

                @pl.when(dy == 0)
                def _():
                    wait(slots.at[0, pl.ds(0, n_x - 1), rows], ga_r.at[phase, half, dy])

                @pl.when(dy != 0)
                def _():
                    wait(g.at[b, pl.ds(0, n_x), core, rows], ga_r.at[phase, half, dy])

            send(group, group, gc_s, gc_r.at[phase, dy], sibling)
            return carry

        def multiply(i, carry):
            dy, b = source(i)
            wait(g.at[b, pl.ds(0, n_x), other], gc_r.at[phase, dy])
            grad = g[b].reshape(block_tiles * TILE, TILE)
            for c in range(n_cb):
                at = pl.ds(c * TILE, TILE)
                acc[at, :] += jnp.dot(dense[b, at, :], grad, preferred_element_type=F32)
            return carry

        lax.fori_loop(0, n_y, pass_on, 0)
        lax.fori_loop(0, n_y, multiply, 0)

    gather(0)
    wait(wslots.at[pl.ds(1, plane - 1)], w2.at[1])
    piece = wt[core, here]
    for k in range(1, plane):
        piece = piece + wslots[k]
    wz[row] = piece
    for dz in strides:
        send(wz.at[row], wz.at[row], w3.at[0], w3.at[1], in_row(dz)[1])

    gather(1)
    for dz in strides:
        rr, device = in_row(dz)
        xs[rr] = acc[pl.ds(pl.multiple_of(rr * zc, 16), zc), :].astype(BF16)
        send(xs.at[rr], xr.at[dz], xsem.at[0], xsem.at[1], device)

    wait(wz.at[pl.ds(0, n_row - 1)], w3.at[1])
    piece = wz[0]
    for k in range(1, n_row):
        piece = piece + wz[k]
    scale = 1.0 / math.sqrt(n_row * n_blocks * block_tiles * TILE)
    final = wo.at[core, here]
    final[...] = piece * scale
    for dy, dx in offsets:
        send(final, final, w5.at[0], w5.at[1], in_plane(dy, dx)[2])
    wait(wo.at[core, pl.ds(0, plane - 1)], w5.at[1])
    send(wo.at[core], wo.at[core], w6.at[0], w6.at[1], sibling)

    total = acc[pl.ds(pl.multiple_of(row * zc, 16), zc), :]
    wait(xr.at[pl.ds(1, n_row - 1)], xsem.at[1])
    for k in range(1, n_row):
        total = total + xr[k].astype(F32)
    ig_out[...] = total.astype(BF16)
    wait(wo.at[other], w6.at[1])
    for c in range(CORES):
        wg_out[c] = wo[c].reshape(TILE, TILE)

    wait(sb, s1s)
    wait(cot.at[zh], csem.at[0])
    wait(slots.at[:, pl.ds(1, plane - 1)], s2s)
    wait(zsend, zs)
    wait(slots.at[:, pl.ds(1, plane - 1)], ga_s)
    wait(sb, gc_s)
    wait(wt.at[other], w1.at[0])
    wait(wslots.at[pl.ds(1, plane - 1)], w2.at[0])
    wait(wz.at[pl.ds(0, n_row - 1)], w3.at[0])
    wait(wo.at[core, pl.ds(0, plane - 1)], w5.at[0])
    wait(wo.at[core], w6.at[0])
    wait(xr.at[pl.ds(1, n_row - 1)], xsem.at[0])


def deliver(act, ig, wg, act_out, ig_out, wg_out, sem):
    copies = [
        pltpu.make_async_copy(act, act_out, sem.at[0]),
        pltpu.make_async_copy(ig, ig_out, sem.at[1]),
    ]
    for c in range(CORES):
        lanes = pl.ds(c * TILE, TILE)
        copies.append(pltpu.make_async_copy(wg.at[c], wg_out.at[:, lanes], sem.at[2 + c]))
    for copy in copies:
        copy.start()
    for copy in copies:
        copy.wait()


def local(tile_values, tile_rows, tile_cols, tile_count, features, weight, cotangent):
    n_row, n_col, n_depth = lax.axis_size("row"), lax.axis_size("col"), lax.axis_size("depth")
    n_y, n_x = n_col // Z_HI, n_depth // CORES
    ch, hid = cotangent.shape
    f = features.shape[1]
    n_cb = features.shape[0] // TILE
    n_blocks = n_col
    block_rows = n_depth * ch
    block_tiles = block_rows // TILE
    slots_max = tile_values.shape[2]
    plane = n_x * n_y
    zc = features.shape[0] // n_row
    piece = f // plane

    sizes = (n_row, n_y, n_x, ch, n_cb, block_tiles, slots_max)
    vmem, dma = pltpu.VMEM, pltpu.SemaphoreType.DMA
    operands = [
        pltpu.with_memory_space_constraint(a, pltpu.HBM)
        for a in (
            tile_rows, tile_cols, tile_values, features.reshape(n_cb, TILE, f),
            weight, cotangent,
        )
    ]
    anywhere = pl.BlockSpec(memory_space=pl.ANY)
    act, ig, wg = pl.pallas_call(
        functools.partial(kernel, sizes),
        out_shape=(
            vmem((ch, hid), BF16),
            vmem((zc, f), BF16),
            vmem((CORES, f, TILE), F32),
        ),
        in_specs=[pl.BlockSpec(memory_space=pltpu.SMEM)]
        + [pl.BlockSpec(memory_space=pltpu.HBM)] * 6,
        out_specs=(pl.BlockSpec(memory_space=pltpu.VMEM),) * 3,
        scratch_shapes=[
            pltpu.SMEM(tile_rows.shape, jnp.int32),
            pltpu.SMEM(tile_cols.shape, jnp.int32),
            vmem((8, TILE), jnp.int32),
            pltpu.SMEM((8, TILE), jnp.int32),
            vmem((slots_max, TILE, TILE), BF16),
            vmem((slots_max + 1, TILE, TILE), BF16),
            vmem((n_cb, TILE, f), BF16),
            vmem(weight.shape, BF16),
            vmem((Z_HI, ch, hid), BF16),
            vmem((Z_HI, ch, hid), BF16),
            vmem((n_blocks, n_cb * TILE, block_rows), BF16),
            vmem((slots_max + 1, TILE, f), F32),
            vmem((n_blocks, block_rows, f), F32),
            vmem((n_blocks, n_x, ch, f), BF16),
            vmem((n_blocks, n_x, ch, f), BF16),
            vmem((n_blocks, n_x, ch, f), BF16),
            vmem((Z_HI, ch, f), F32),
            vmem((Z_HI, plane, ch, f), BF16),
            vmem((Z_HI, ch, f), BF16),
            vmem((Z_HI, ch, f), BF16),
            vmem((n_blocks, n_x, CORES, ch, f), BF16),
            vmem((n_cb * TILE, f), F32),
            vmem((n_row, zc, f), BF16),
            vmem((n_row, zc, f), BF16),
            vmem((CORES, plane, piece, TILE), F32),
            vmem((plane, piece, TILE), F32),
            vmem((plane, piece, TILE), F32),
            vmem((n_row, piece, TILE), F32),
            vmem((CORES, plane, piece, TILE), F32),
            dma((2,)),
            dma,
            dma((LOADS + 3,)),
            dma((2,)),
            dma,
            dma((n_blocks,)),
            dma,
            dma((Z_HI, 2)),
            dma,
            dma((Z_HI, 2)),
            dma,
            dma((Z_HI, 2, n_y)),
            dma,
            dma((Z_HI, n_y)),
            dma((2,)),
            dma((2,)),
            dma((2,)),
            dma((2,)),
            dma((2,)),
            dma((2,)),
        ],
        compiler_params=pltpu.CompilerParams(
            collective_id=0, has_side_effects=True, vmem_limit_bytes=40 * 1024 * 1024
        ),
        name="graph_layer",
    )(tile_count, *operands)
    act, ig, weight_grad = pl.pallas_call(
        deliver,
        out_shape=(
            jax.ShapeDtypeStruct((ch, hid), BF16),
            jax.ShapeDtypeStruct((zc, f), BF16),
            jax.ShapeDtypeStruct((f, hid), F32),
        ),
        in_specs=[pl.BlockSpec(memory_space=pltpu.VMEM)] * 3,
        out_specs=(pl.BlockSpec(memory_space=pltpu.HBM),) * 3,
        scratch_shapes=[dma((2 + CORES,))],
        name="deliver",
    )(*[pltpu.with_memory_space_constraint(a, pltpu.VMEM) for a in (act, ig, wg)])
    return act, ig[None], weight_grad


def solution(mesh):
    in_specs = (
        P("row", ("col", "depth"), None, None, None),
        P("row", ("col", "depth"), None),
        P("row", ("col", "depth"), None),
        P("row", ("col", "depth")),
        P(("col", "depth"), None),
        P(),
        P(("row", "col", "depth"), None),
    )
    out_specs = (P(("row", "col", "depth"), None), P(("col", "depth"), "row", None), P())
    return jax.shard_map(local, mesh=mesh, in_specs=in_specs, out_specs=out_specs, check_vma=False)
```
